128 devices in a mesh: expert: 32 (over y_hi, z, x), width: 4 (over y_lo, core).
Axes of the slice: x: 4, y: 4 (y_hi: 2, y_lo: 2; y = y_hi * 2 + y_lo), z: 4, core: 2. Of those that a mesh axis runs over, the one named last changes fastest.
Arguments:
- tokens: bfloat16 [4096, 2880], P('expert', 'width'), may hold values from -6 to 6
- grad_out: bfloat16 [4096, 2880], P('expert', 'width'), may hold values from -6 to 6
- routes: int32 [4096, 4], P('expert'), may hold values from 0 to 127, all different within a row; in each aligned block of 128 rows (0 to 127, 128 to 255, ...) at most 5 rows name the same one
- gates: float32 [4096, 4], P('expert'), may hold values from 0.05 to 1
- ranks: int32 [128], P('expert'), may hold values from 64 to 512
- w_gate: bfloat16 [2880, 2880], P('expert', 'width'), may hold values from -0.109375 to 0.109375
- w_up: bfloat16 [2880, 2880], P('expert', 'width'), may hold values from -0.109375 to 0.109375
- w_down: bfloat16 [2880, 2880], P('width', 'expert'), may hold values from -0.109375 to 0.109375
- delta_in: bfloat16 [128, 2880, 512], P('expert', 'width'), may hold values from -0.109375 to 0.109375
- delta_out: bfloat16 [128, 512, 2, 2880], P('expert', None, None, 'width'), may hold values from -0.25 to 0.25
Outputs:
- grad_tokens: bfloat16 [4096, 2880], P('expert', 'width')
- grad_gate: bfloat16 [2880, 2880], P('expert', 'width')
- grad_up: bfloat16 [2880, 2880], P('expert', 'width')
- grad_down: bfloat16 [2880, 2880], P('width', 'expert')
- grad_delta_in: bfloat16 [128, 2880, 512], P('expert', 'width')
- grad_delta_out: bfloat16 [128, 512, 2, 2880], P('expert', None, None, 'width')
The draws below stay inside these ranges and needn't reach their ends.
Inputs may be any that keep to these rules, and one draw needn't show every extreme that they name: `routes`: each row names 4 different experts; among the 128 rows of one index of the expert axis (aligned blocks) no expert is named by more than 5 rows, a bound that some block reaches in every draw.
All inputs are finite; a program needn't handle non-finite values.
Results may differ from the reference program's by a relative error of at most 0.03.
Values may be sent and summed in bfloat16 or wider, within the bound.
No kernel may reach another device: no remote copies, remote signals or barrier semaphores. Data moves between devices by JAX's collectives and lax.ppermute only.
A program may use at most 128 MiB of HBM per device.

```python
import math
import jax
import jax.numpy as jnp
import numpy as np
from jax import lax

D = 2880
FF = 2880
TOPK = 4
RMAX = 512
TOK_DEV = 128
EXPERTS = 128
TOKENS = 4096
CAP = 5
N_EXPERT = 32


def with_ends(values, stream_key, low, high):
    longest = values.shape.index(max(values.shape))
    spots = []
    for shift in (0, 1):
        where = [jax.random.randint(jax.random.fold_in(stream_key, axis), (), 0, length) for axis, length in enumerate(values.shape)]
        where[longest] = (where[longest] + shift) % values.shape[longest]
        spots.append(tuple(where))
    return values.at[spots[0]].set(low).at[spots[1]].set(high)


def strengthened(entries, rng, source, target, shards_of, factor):
    owner, partner = [(jnp.arange(entries.shape[position]) // (entries.shape[position] // shards_of)).reshape([-1 if axis == position else 1 for axis in range(entries.ndim)]) for position in (source, target)]
    chosen = jax.random.permutation(rng, shards_of)[partner]
    strong = (owner == chosen) | (owner == (partner + shards_of // 2) % shards_of)
    return jnp.where(strong, factor * entries, entries)


def block_scale(stream_key, shape, split, low, largest):
    level = 1.0
    for position, parts in split:
        heights = jax.random.uniform(jax.random.fold_in(jax.random.fold_in(stream_key, 6), position), (parts,), jnp.float32, low / len(split), largest / len(split))
        level = level * jnp.repeat(jnp.exp(heights), shape[position] // parts).reshape((-1,) + (1,) * (len(shape) - 1 - position))
    return level


def shared_out(key, own, number, rows, count, top, bound, lean):
    order = jax.random.permutation(key, count)
    heavy_load, usual = shares(count, rows * top, bound, lean, True), shares(count, rows * top, bound, lean, False)
    places = jnp.arange(count)

    def named(tallies, turn):
        used = int((tallies > 0).sum())
        fixed = max(1, used // 4)
        passed = fixed + (places - fixed + turn * (used - fixed)) % max(1, count - fixed)
        return jnp.zeros((count,), jnp.int32).at[order[jnp.where(places < fixed, places, passed)]].set(jnp.asarray(tallies, jnp.int32))

    tallies = jnp.where(number % 4 == 0, named(heavy_load, number // 4), named(usual, number - number // 4 - 1))
    mixed = jax.random.permutation(jax.random.fold_in(own, 3), count)
    donor, taker = mixed[0:count // 2 * 2:2], mixed[1:count // 2 * 2:2]
    room = jnp.minimum(tallies[donor] - 1, bound - tallies[taker]) // 2
    room = jnp.where((donor == order[0]) | (taker == order[0]) | (tallies[taker] == 0), 0, jnp.maximum(room, 0))
    passed = jax.random.randint(jax.random.fold_in(own, 4), (count // 2,), 0, 1 << 20) % (room + 1)
    tallies = tallies.at[donor].add(-passed).at[taker].add(passed)
    items = jnp.searchsorted(jnp.cumsum(tallies), jnp.arange(rows * top), side="right").astype(jnp.int32)
    grid = items.reshape(top, rows).T
    grid = grid[jax.random.permutation(jax.random.fold_in(own, 1), rows)]
    turn = jax.random.randint(jax.random.fold_in(own, 2), (rows, 1), 0, top)
    return jnp.take_along_axis(grid, (jnp.arange(top)[None, :] + turn) % top, axis=1)


def shares(amount, total, reach, slope, full):
    portions = [(1 << 20) // math.isqrt(standing ** slope) + 1 for standing in range(1, amount + 1)]
    largest = reach if full else min(reach, max(-(-total // amount), total * portions[0] // sum(portions)))
    least = 1 if total - largest >= amount - 1 else 0
    holding, surplus = [largest] + [least] * (amount - 1), total - largest - least * (amount - 1)
    while surplus > 0:
        movable = [i for i in range(1, amount) if holding[i] < largest] or [i for i in range(1, amount) if holding[i] < reach]
        whole, left = sum([portions[i] for i in movable]), surplus
        for i in movable:
            more = min(reach - holding[i], max(1, left * portions[i] // whole), surplus)
            holding[i] = holding[i] + more
            surplus = surplus - more
    return np.array(holding)


def scatter_about(stream_key, shape, deviation, most, cuts=(), kind=jnp.bfloat16):
    loudness = block_scale(stream_key, shape, cuts, -0.22, 0.18) if cuts else 1.0
    result = jax.random.normal(stream_key, shape, jnp.float32) * deviation * loudness
    return jnp.minimum(jnp.maximum(result, -most), most).astype(kind)


def bell_draw_with(rng, shape, deviation, reach, pieces, heavy, kind=jnp.bfloat16):
    array = deviation * jax.random.normal(rng, shape, jnp.float32)
    if pieces:
        array = array * block_scale(rng, shape, pieces, -0.22, 0.18)
    return jnp.clip(strengthened(array, jax.random.fold_in(rng, 3), *heavy), -reach, reach).astype(kind)


def setup_inputs(seed: int = 0) -> dict:
    key_of = jax.random.split(jax.random.key(seed), 11)
    tokens = bell_draw_with(key_of[0], (TOKENS, D), 1.0, 6.0, ((0, 32), (1, 4)), (0, 1, 32, 2.75))
    grad_out = bell_draw_with(key_of[1], (TOKENS, D), 1.0, 6.0, ((0, 32), (1, 4)), (0, 1, 32, 2.75))
    routes_keys = jax.random.split(jax.random.fold_in(key_of[2], 1), TOKENS // TOK_DEV)
    routes_turns = jax.random.permutation(jax.random.fold_in(key_of[2], 3), TOKENS // TOK_DEV)
    routes = jax.vmap(lambda own, number: shared_out(jax.random.fold_in(key_of[2], 2), own, number, TOK_DEV, EXPERTS, TOPK, CAP, 2))(routes_keys, routes_turns).reshape((TOKENS, TOPK))
    gates = jnp.clip(0.05 + 0.95 * jax.random.uniform(key_of[3], (TOKENS, TOPK), jnp.float32) ** block_scale(key_of[3], (TOKENS, TOPK), ((0, 32),), -0.2, 0.2), 0.05, 1.0)
    ranks = with_ends(jax.random.randint(key_of[4], (EXPERTS,), RMAX // 8, RMAX + 1), jax.random.fold_in(key_of[4], 1), RMAX // 8, RMAX).astype(jnp.int32)
    w_gate = scatter_about(key_of[5], (D, FF), D ** -0.5, 0.109375, ((0, 32), (1, 4)))
    w_up = scatter_about(key_of[6], (D, FF), D ** -0.5, 0.109375, ((0, 32), (1, 4)))
    w_down = scatter_about(key_of[7], (FF, D), FF ** -0.5, 0.109375, ((0, 4), (1, 32)))
    delta_in = scatter_about(key_of[8], (EXPERTS, D, RMAX), D ** -0.5, 0.109375, ((0, 32), (1, 4)))
    delta_out = scatter_about(key_of[9], (EXPERTS, RMAX, 2, FF), RMAX ** -0.5, 0.25, ((0, 32), (3, 4)))
    return {"tokens": tokens, "grad_out": grad_out, "routes": routes, "gates": gates, "ranks": ranks, "w_gate": w_gate, "w_up": w_up, "w_down": w_down, "delta_in": delta_in, "delta_out": delta_out}


def rounded(values):
    return lax.optimization_barrier(values.astype(jnp.bfloat16)).astype(jnp.float32)


def reference(tokens, grad_out, routes, gates, ranks, w_gate, w_up, w_down, delta_in, delta_out):
    precise = lax.Precision.HIGHEST
    base_gate = rounded(jnp.dot(tokens, w_gate, preferred_element_type=jnp.float32))
    base_up = rounded(jnp.dot(tokens, w_up, preferred_element_type=jnp.float32))
    down_grad = jnp.dot(grad_out, w_down.T, preferred_element_type=jnp.float32)
    flat_routes = routes.reshape(-1).astype(jnp.int32)
    pair_count = flat_routes.shape[0]
    sorted_pairs = jnp.argsort(flat_routes, stable=True).astype(jnp.int32)
    expert_counts = jnp.sum((flat_routes[:, None] == jnp.arange(EXPERTS, dtype=jnp.int32)[None, :]).astype(jnp.int32), axis=0)
    expert_starts = jnp.cumsum(expert_counts) - expert_counts
    slot_rows = N_EXPERT * CAP
    flat_gates = gates.reshape(-1)
    rank_index = jnp.arange(RMAX, dtype=jnp.int32)

    def one_expert(totals, expert_id):
        mixed_acc, summed_acc, back_acc = totals
        slot_pos = jnp.arange(slot_rows, dtype=jnp.int32)
        filled = (slot_pos < expert_counts[expert_id]).astype(jnp.float32)
        pair_index = sorted_pairs[jnp.clip(expert_starts[expert_id] + slot_pos, 0, pair_count - 1)]
        token_index = (pair_index // TOPK).astype(jnp.int32)
        gate_value = flat_gates[pair_index] * filled
        rows_x = tokens[token_index].astype(jnp.float32)
        rank_mask = (rank_index < ranks[expert_id]).astype(jnp.float32)
        factor_in = delta_in[expert_id].astype(jnp.float32)
        factor_out = delta_out[expert_id].astype(jnp.float32)
        low_rank = rounded(jnp.dot(rows_x, factor_in, precision=precise) * rank_mask[None, :])
        activation = base_gate[token_index] + jnp.dot(low_rank, factor_out[:, 0, :], precision=precise)
        up_value = base_up[token_index] + jnp.dot(low_rank, factor_out[:, 1, :], precision=precise)
        sigmoid_act = jax.nn.sigmoid(activation)
        swish_value = activation * sigmoid_act
        hidden = rounded(swish_value * up_value)
        pair_down = rounded(gate_value[:, None] * down_grad[token_index])
        grad_act = rounded(pair_down * up_value * sigmoid_act * (1.0 + activation * (1.0 - sigmoid_act)))
        grad_upper = rounded(pair_down * swish_value)
        pair_grad = jnp.stack([grad_act, grad_upper], axis=1)
        out_factor = jnp.einsum("rk,rcf->kcf", low_rank, pair_grad, precision=precise).astype(jnp.bfloat16)
        back_sum = jnp.einsum("rcf,kcf->rk", pair_grad, factor_out, precision=precise)
        low_grad = rounded(back_sum * rank_mask[None, :])
        in_factor = jnp.dot(rows_x.T, low_grad, precision=precise).astype(jnp.bfloat16)
        back_rows = rounded(jnp.dot(low_grad, factor_in.T, precision=precise))
        mixed_acc = mixed_acc.at[token_index].add(gate_value[:, None] * hidden)
        summed_acc = summed_acc.at[token_index].add(filled[:, None] * jnp.concatenate([grad_act, grad_upper], axis=1))
        back_acc = back_acc.at[token_index].add(filled[:, None] * back_rows)
        return (mixed_acc, summed_acc, back_acc), (in_factor, out_factor)

    initial = (jnp.zeros((TOKENS, FF), jnp.float32), jnp.zeros((TOKENS, 2 * FF), jnp.float32), jnp.zeros((TOKENS, D), jnp.float32))
    accums, factors = lax.scan(one_expert, initial, jnp.arange(EXPERTS, dtype=jnp.int32))
    mixed_acc, summed_acc, back_acc = accums
    grad_delta_in, grad_delta_out = factors
    mixed_hidden = rounded(mixed_acc)
    summed = rounded(summed_acc)
    weight_both = jnp.concatenate([w_gate, w_up], axis=1).astype(jnp.float32)
    grad_tokens = (jnp.dot(summed, weight_both.T, precision=precise) + back_acc).astype(jnp.bfloat16)

    def block_sum(totals, block_data):
        x_block, dy_block, mixed_block, summed_block = block_data
        gate_part = rounded(jnp.dot(x_block.astype(jnp.float32).T, summed_block, precision=precise))
        down_part = rounded(jnp.dot(mixed_block.T, dy_block.astype(jnp.float32), precision=precise))
        return (totals[0] + gate_part, totals[1] + down_part), None

    blocks = (tokens.reshape(N_EXPERT, TOK_DEV, D), grad_out.reshape(N_EXPERT, TOK_DEV, D),
              mixed_hidden.reshape(N_EXPERT, TOK_DEV, FF), summed.reshape(N_EXPERT, TOK_DEV, 2 * FF))
    start_sums = (jnp.zeros((D, 2 * FF), jnp.float32), jnp.zeros((FF, D), jnp.float32))
    grad_sums, unused = lax.scan(block_sum, start_sums, blocks)
    grad_gate = grad_sums[0][:, :FF].astype(jnp.bfloat16)
    grad_up = grad_sums[0][:, FF:].astype(jnp.bfloat16)
    grad_down = grad_sums[1].astype(jnp.bfloat16)
    return (grad_tokens, grad_gate, grad_up, grad_down, grad_delta_in, grad_delta_out)
```

```python
import jax
import jax.numpy as jnp
from jax import lax
from jax.sharding import Mesh, PartitionSpec as P

BF = jnp.bfloat16
F32 = jnp.float32
EXPERT = ("yh", "z", "x")
PLANE = ("z", "x")
WIDTH = ("yl", "c")
COLUMN = ("yh", "yl", "c")
CAP = 5
HALF = 384


def dot(a, b, dims):
    return lax.dot_general(a, b, (dims, ((), ())), preferred_element_type=F32)


def bdot(a, b, dims):
    return lax.dot_general(a, b, (dims, ((0,), (0,))), preferred_element_type=F32)


def targets_of(routes, experts):
    flat = routes.reshape(-1, 1)
    pairs = flat.shape[0]
    onehot = (flat == lax.broadcasted_iota(jnp.int32, (pairs, experts), 1)).astype(BF)
    earlier = lax.broadcasted_iota(jnp.int32, (pairs, pairs), 0) > lax.broadcasted_iota(
        jnp.int32, (pairs, pairs), 1
    )
    before = dot(earlier.astype(BF), onehot, ((1,), (0,)))
    place = jnp.sum(before * onehot.astype(F32), axis=1).astype(jnp.int32)
    return (flat[:, 0] * CAP + place).reshape(routes.shape)


def width_sum(partial, mask):
    parts = lax.all_to_all(partial.astype(BF), WIDTH, 0, 0)
    total = jnp.sum(parts.astype(F32), axis=0)
    mine = (total * mask).astype(BF)
    return lax.all_gather(mine, WIDTH)


def pad_cols(a):
    return jnp.pad(a, ((0, 0),) * (a.ndim - 1) + ((0, 2 * HALF - a.shape[-1]),))


def local(tokens, grad_out, routes, gates, ranks, w_gate, w_up, w_down, delta_in, delta_out):
    yh = lax.axis_index("yh")
    wi = lax.axis_index("yl") * 2 + lax.axis_index("c")
    rows, part = tokens.shape
    local_e, _, rank_max = delta_in.shape
    n_exp = 32
    experts = n_exp * local_e
    per_dev = local_e * CAP
    slots = experts * CAP
    er = n_exp * CAP
    wr = w_gate.shape[0]

    w3 = jnp.stack([pad_cols(w_gate), pad_cols(w_up), pad_cols(w_down.T)], axis=1)
    keep = lax.dynamic_slice_in_dim(w3, yh * HALF, HALF, 2).reshape(wr, 3 * HALF)
    give = lax.dynamic_slice_in_dim(w3, (1 - yh) * HALF, HALF, 2).reshape(wr, 3 * HALF)
    got = lax.ppermute(give, "yh", [(0, 1), (1, 0)])
    both = jnp.where(yh == 0, jnp.stack([keep, got]), jnp.stack([got, keep]))
    full = lax.all_gather(both, PLANE)
    full = full.transpose(1, 0, 2, 3).reshape(4, part, 3 * HALF)

    xy = lax.all_gather(jnp.stack([tokens, grad_out]), COLUMN)
    xy = xy.reshape(2, 4, 2, rows, part)
    xs = [jnp.concatenate([xy[0, w, 0], xy[1, w, 0]], axis=0) for w in range(4)]
    ys = [jnp.concatenate([xy[0, w, 1], xy[1, w, 1]], axis=0) for w in range(4)]

    target = targets_of(routes, experts)
    slot_ids = lax.broadcasted_iota(jnp.int32, (slots, rows), 0)
    picker = sum((target[None, :, k] == slot_ids).astype(F32) for k in range(4)).astype(BF)
    target2 = lax.all_gather(target, "yh")
    gates2 = lax.all_gather(gates, "yh")
    block_of = lax.broadcasted_iota(jnp.int32, (2, rows, 4), 0)
    place2 = (target2 // per_dev) * (2 * per_dev) + block_of * per_dev + target2 % per_dev
    place2 = place2.reshape(2 * rows, 4)
    gates2 = gates2.reshape(2 * rows, 4)
    ids2 = lax.broadcasted_iota(jnp.int32, (2 * slots, 2 * rows), 0)
    hits = [place2[None, :, k] == ids2 for k in range(4)]
    picker2 = sum(h.astype(F32) for h in hits).astype(BF)
    gate_slot = jnp.sum(
        sum(jnp.where(h, gates2[None, :, k], 0.0) for k, h in enumerate(hits)), axis=1, keepdims=True
    )

    r_exp = lax.broadcasted_iota(jnp.int32, (slots, slots), 0)
    s_in = lax.broadcasted_iota(jnp.int32, (slots, slots), 1)
    e_r, zx_r, b_r, p_r = r_exp // er, (r_exp % er) // (2 * CAP), (r_exp % (2 * CAP)) // CAP, r_exp % CAP
    perm_x = (s_in == (b_r * 16 + zx_r) * per_dev + e_r * CAP + p_r).astype(BF)
    perm_p = (s_in == (zx_r * 2 + b_r) * per_dev + e_r * CAP + p_r).astype(BF)

    out_x = dot(picker, tokens, ((1,), (0,))).astype(BF).reshape(n_exp, per_dev, part)
    in_x = lax.all_to_all(out_x, EXPERT, 0, 0).reshape(slots, part)
    rows_x = dot(perm_x, in_x, ((1,), (0,))).astype(BF).reshape(local_e, er, part)
    rank_ids = lax.broadcasted_iota(jnp.int32, (1, rank_max), 1)
    mask = (rank_ids < ranks[wi]).astype(F32)
    low = width_sum(bdot(rows_x, delta_in, ((2,), (1,))), mask)
    halves = []
    for h in range(2):
        cols = []
        for c in range(2):
            d = bdot(low, delta_out[:, :, c, h * HALF : min(part, (h + 1) * HALF)], ((2,), (1,)))
            d = d.astype(BF)
            if h == 1:
                d = jnp.pad(d, ((0, 0), (0, 0), (0, 2 * HALF - part)))
            cols.append(d)
        cols = jnp.concatenate(cols, axis=2).reshape(slots, 2 * HALF)
        halves.append(dot(perm_p, cols, ((0,), (0,))).astype(BF).reshape(16, 2 * per_dev, 2 * HALF))
    back_pre = lax.all_to_all(jnp.concatenate(halves, axis=0), EXPERT, 0, 0)
    back_pre = back_pre.reshape(2 * slots, 2 * HALF)

    base = sum(dot(xs[w], full[w, :, : 2 * HALF], ((1,), (0,))) for w in range(4)).astype(BF)
    down = sum(dot(ys[w], full[w, :, 2 * HALF :], ((1,), (0,))) for w in range(4)).astype(BF)
    pre = dot(picker2, base, ((1,), (0,))) + back_pre.astype(F32)
    pair_down = (gate_slot * dot(picker2, down, ((1,), (0,)))).astype(BF).astype(F32)
    act, up = pre[:, :HALF], pre[:, HALF:]
    sig = jax.nn.sigmoid(act)
    swish = act * sig
    weighted = (gate_slot * (swish * up)).astype(BF)
    grad_act = pair_down * up * sig * (1.0 + act * (1.0 - sig))
    grad_up_ = pair_down * swish
    pair_grad = jnp.concatenate([grad_act, grad_up_], axis=1).astype(BF)
    mixed = dot(picker2, weighted, ((0,), (0,))).astype(BF)
    summed = dot(picker2, pair_grad, ((0,), (0,))).astype(BF)

    dw = jnp.stack(
        [
            jnp.concatenate(
                [dot(xs[w], summed, ((0,), (0,))), dot(ys[w], mixed, ((0,), (0,)))], axis=1
            ).astype(BF)
            for w in range(4)
        ]
    )
    dw = dw.reshape(2, 16, wr, 3 * HALF).transpose(1, 0, 2, 3).reshape(16, 2 * wr, 3 * HALF)
    dw = lax.psum_scatter(dw, PLANE).reshape(2, wr, 3 * HALF)
    mine = lax.dynamic_index_in_dim(dw, yh, 0, keepdims=False)
    other = lax.dynamic_index_in_dim(dw, 1 - yh, 0, keepdims=False)
    other = lax.ppermute(other, "yh", [(0, 1), (1, 0)])
    lo = jnp.where(yh == 0, mine, other)
    hi = jnp.where(yh == 0, other, mine)
    rest = part - HALF
    grads = [
        jnp.concatenate([lo[:, i * HALF : (i + 1) * HALF], hi[:, i * HALF : i * HALF + rest]], axis=1)
        for i in range(3)
    ]

    in_p = lax.all_to_all(pair_grad.reshape(n_exp, 2 * per_dev, 2 * HALF), EXPERT, 0, 0)
    in_p = in_p.reshape(2, slots, 2 * HALF)
    pg = [dot(perm_p, in_p[h], ((1,), (0,))).astype(BF) for h in range(2)]
    pg = jnp.stack(
        [
            jnp.concatenate([pg[0][:, c * HALF : (c + 1) * HALF], pg[1][:, c * HALF : c * HALF + rest]], axis=1)
            for c in range(2)
        ],
        axis=1,
    ).reshape(local_e, er, 2, part)
    low_back = lax.dot_general(
        pg, delta_out, (((2, 3), (2, 3)), ((0,), (0,))), preferred_element_type=F32
    )
    low_grad = width_sum(low_back, mask)
    grad_delta_out = lax.dot_general(
        low, pg, (((1,), (1,)), ((0,), (0,))), preferred_element_type=F32
    ).astype(BF)
    grad_delta_in = bdot(rows_x, low_grad, ((1,), (1,))).astype(BF)
    back = bdot(low_grad, delta_in, ((2,), (2,))).astype(BF).reshape(slots, part)
    back = dot(perm_x, back, ((0,), (0,))).astype(BF).reshape(n_exp, per_dev, part)
    back = lax.all_to_all(back, EXPERT, 0, 0).reshape(slots, part)
    token_back = dot(picker, back, ((0,), (0,)))

    dx = jnp.stack([dot(summed, full[w, :, : 2 * HALF], ((1,), (1,))) for w in range(4)]).astype(BF)
    dx = dx.reshape(4, 2, rows, part).transpose(1, 0, 2, 3).reshape(8, rows, part)
    dx = lax.psum_scatter(dx, COLUMN).astype(F32)
    grad_tokens = (dx + token_back).astype(BF)
    return (grad_tokens, grads[0], grads[1], grads[2].T, grad_delta_in, grad_delta_out)


def solution(mesh):
    fine = Mesh(mesh.devices.reshape(2, 4, 4, 2, 2), ("yh", "z", "x", "yl", "c"))
    return jax.shard_map(
        local,
        mesh=fine,
        in_specs=(
            P(EXPERT, WIDTH),
            P(EXPERT, WIDTH),
            P(EXPERT, None),
            P(EXPERT, None),
            P(EXPERT),
            P(EXPERT, WIDTH),
            P(EXPERT, WIDTH),
            P(WIDTH, EXPERT),
            P(EXPERT, WIDTH, None),
            P(EXPERT, None, None, WIDTH),
        ),
        out_specs=(
            P(EXPERT, WIDTH),
            P(EXPERT, WIDTH),
            P(EXPERT, WIDTH),
            P(WIDTH, EXPERT),
            P(EXPERT, WIDTH, None),
            P(EXPERT, None, None, WIDTH),
        ),
        check_vma=False,
    )
```

```python
import jax
import jax.numpy as jnp
from jax import lax
from jax.sharding import Mesh, PartitionSpec as P

BF = jnp.bfloat16
F32 = jnp.float32
EXPERT = ("yh", "z", "x")
PLANE = ("z", "x")
WIDTH = ("yl", "c")
COLUMN = ("yh", "yl", "c")
CAP = 5
HALF = 384
PADDED = 96
WPART = 768
XROWS = 24


def dot(a, b, dims):
    return lax.dot_general(a, b, (dims, ((), ())), preferred_element_type=F32)


def bdot(a, b, dims):
    return lax.dot_general(a, b, (dims, ((0,), (0,))), preferred_element_type=F32)


def targets_of(routes_t, experts):
    flat = routes_t.reshape(1, -1)
    pairs = flat.shape[1]
    onehot = (flat == lax.broadcasted_iota(jnp.int32, (experts, pairs), 0)).astype(BF)
    earlier = lax.broadcasted_iota(jnp.int32, (pairs, pairs), 0) < lax.broadcasted_iota(
        jnp.int32, (pairs, pairs), 1
    )
    before = dot(onehot, earlier.astype(BF), ((1,), (0,)))
    place = jnp.sum(before * onehot.astype(F32), axis=0).astype(jnp.int32)
    return place.reshape(routes_t.shape)


def width_sum(partial, mask):
    parts = lax.all_to_all(partial.astype(BF), WIDTH, 0, 0)
    total = jnp.sum(parts.astype(F32), axis=0)
    mine = (total * mask).astype(BF)
    return lax.all_gather(mine, WIDTH)


def pad_cols(a):
    return jnp.pad(a, ((0, 0),) * (a.ndim - 1) + ((0, 2 * HALF - a.shape[-1]),))


def swap_y(a):
    return lax.ppermute(a, "yh", [(0, 1), (1, 0)])


def local(tokens, grad_out, routes, gates, ranks, w_gate, w_up, w_down, delta_in, delta_out):
    yh = lax.axis_index("yh")
    wi = lax.axis_index("yl") * 2 + lax.axis_index("c")
    rows, part = tokens.shape
    local_e, _, rank_max = delta_in.shape
    n_exp = 32
    experts = n_exp * local_e
    slots = experts * CAP
    er = n_exp * CAP
    wr = w_gate.shape[0]
    rest = part - HALF

    d_id = lax.broadcasted_iota(jnp.int32, (part, WPART), 0)
    j_id = lax.broadcasted_iota(jnp.int32, (part, WPART), 1)
    spread = ((d_id // wr == j_id // PADDED) & (d_id % wr == j_id % PADDED)).astype(BF)

    w3 = jnp.stack([pad_cols(w_gate), pad_cols(w_up), pad_cols(w_down.T)], axis=1)
    w3 = jnp.pad(w3, ((0, PADDED - wr), (0, 0), (0, 0)))
    keep = lax.dynamic_slice_in_dim(w3, yh * HALF, HALF, 2).reshape(PADDED, 3 * HALF)
    give = lax.dynamic_slice_in_dim(w3, (1 - yh) * HALF, HALF, 2).reshape(PADDED, 3 * HALF)
    own_w = lax.all_gather(keep, PLANE).reshape(2 * WPART, 3 * HALF)
    far_w = lax.all_gather(swap_y(give), PLANE).reshape(2 * WPART, 3 * HALF)

    place = targets_of(routes.T, experts)
    routes_t, gates_t = routes.T, gates.T
    info = jnp.concatenate([(routes_t * 8 + place).astype(F32), gates_t], axis=0)
    far = swap_y(info)
    info2 = jnp.where(
        yh == 0, jnp.concatenate([info, far], axis=1), jnp.concatenate([far, info], axis=1)
    )
    target = (routes_t // local_e) * XROWS + (routes_t % local_e) * CAP + place
    slot_ids = lax.broadcasted_iota(jnp.int32, (n_exp * XROWS, rows), 0)
    picker = sum((target[k : k + 1] == slot_ids).astype(F32) for k in range(4)).astype(BF)

    out_x = dot(picker, tokens, ((1,), (0,))).astype(BF).reshape(n_exp, XROWS, part)
    in_x = lax.all_to_all(out_x, EXPERT, 0, 0).reshape(n_exp * XROWS, part)

    xy = jnp.stack([dot(tokens, spread, ((1,), (0,))), dot(grad_out, spread, ((1,), (0,)))]).astype(BF)
    xy = lax.all_gather(xy, COLUMN).reshape(2, 4, 2, rows, WPART)

    def feats(first, which):
        two = lax.dynamic_slice_in_dim(xy[:, :, which], first, 2, 1)
        return two.transpose(0, 2, 1, 3).reshape(2 * rows, 2 * WPART)

    own_x, far_x, own_y, far_y = [feats(f, k) for k in (0, 1) for f in (2 * yh, 2 - 2 * yh)]

    def order(width, source):
        r = lax.broadcasted_iota(jnp.int32, (slots, width), 0)
        s_in = lax.broadcasted_iota(jnp.int32, (slots, width), 1)
        return (s_in == source(r // er, (r % er) // (2 * CAP), (r % (2 * CAP)) // CAP, r % CAP)).astype(BF)

    perm_x = order(n_exp * XROWS, lambda e, zx, b, p: (b * 16 + zx) * XROWS + e * CAP + p)
    perm_p = order(slots, lambda e, zx, b, p: (zx * 2 + b) * (local_e * CAP) + e * CAP + p)
    rows_x = dot(perm_x, in_x, ((1,), (0,))).astype(BF).reshape(local_e, er, part)
    rank_ids = lax.broadcasted_iota(jnp.int32, (1, rank_max), 1)
    mask = (rank_ids < ranks[wi]).astype(F32)
    low = width_sum(bdot(rows_x, delta_in, ((2,), (1,))), mask)
    halves = []
    for h in range(2):
        cols = []
        for c in range(2):
            d = bdot(low, delta_out[:, :, c, h * HALF : min(part, (h + 1) * HALF)], ((2,), (1,)))
            d = d.astype(BF)
            if h == 1:
                d = jnp.pad(d, ((0, 0), (0, 0), (0, 2 * HALF - part)))
            cols.append(d)
        cols = jnp.concatenate(cols, axis=2).reshape(slots, 2 * HALF)
        halves.append(dot(perm_p, cols, ((0,), (0,))).astype(BF).reshape(16, 2 * local_e * CAP, 2 * HALF))
    back_pre = lax.all_to_all(jnp.concatenate(halves, axis=0), EXPERT, 0, 0)
    back_pre = back_pre.reshape(2 * slots, 2 * HALF)

    coded = info2[:4].astype(jnp.int32)
    route2, place2 = coded // 8, coded % 8
    block2 = lax.broadcasted_iota(jnp.int32, (4, 2 * rows), 1) // rows
    target2 = ((route2 // local_e) * 2 + block2) * (local_e * CAP) + (route2 % local_e) * CAP + place2
    ids2 = lax.broadcasted_iota(jnp.int32, (2 * slots, 2 * rows), 0)
    hits = [target2[k : k + 1] == ids2 for k in range(4)]
    picker2 = sum(h.astype(F32) for h in hits).astype(BF)
    gate_slot = jnp.sum(
        sum(jnp.where(h, info2[4 + k : 5 + k], 0.0) for k, h in enumerate(hits)), axis=1, keepdims=True
    )

    own_gu, own_d, far_gu, far_d = own_w[:, : 2 * HALF], own_w[:, 2 * HALF :], far_w[:, : 2 * HALF], far_w[:, 2 * HALF :]
    base = (dot(own_x, own_gu, ((1,), (0,))) + dot(far_x, far_gu, ((1,), (0,)))).astype(BF)
    down = (dot(own_y, own_d, ((1,), (0,))) + dot(far_y, far_d, ((1,), (0,)))).astype(BF)
    pre = dot(picker2, base, ((1,), (0,))) + back_pre.astype(F32)
    pair_down = (gate_slot * dot(picker2, down, ((1,), (0,)))).astype(BF).astype(F32)
    act, up = pre[:, :HALF], pre[:, HALF:]
    sig = jax.nn.sigmoid(act)
    swish = act * sig
    weighted = (gate_slot * (swish * up)).astype(BF)
    grad_act = pair_down * up * sig * (1.0 + act * (1.0 - sig))
    grad_up_ = pair_down * swish
    pair_grad = jnp.concatenate([grad_act, grad_up_], axis=1).astype(BF)
    in_p = lax.all_to_all(pair_grad.reshape(n_exp, 2 * local_e * CAP, 2 * HALF), EXPERT, 0, 0)
    in_p = in_p.reshape(2, slots, 2 * HALF)
    mixed = dot(picker2, weighted, ((0,), (0,))).astype(BF)
    summed = dot(picker2, pair_grad, ((0,), (0,))).astype(BF)

    def plane_sum(feat, grad):
        dw = dot(feat, grad, ((0,), (0,))).astype(BF)
        return lax.psum_scatter(dw.reshape(16, PADDED, -1), PLANE)

    other_x, other_y = plane_sum(far_x, summed), plane_sum(far_y, mixed)
    mine_x, mine_y = plane_sum(own_x, summed), plane_sum(own_y, mixed)
    other = swap_y(jnp.concatenate([other_x, other_y], axis=1))
    mine = jnp.concatenate([mine_x, mine_y], axis=1)
    lo = jnp.where(yh == 0, mine, other)[:wr]
    hi = jnp.where(yh == 0, other, mine)[:wr]
    grads = [
        jnp.concatenate([lo[:, i * HALF : (i + 1) * HALF], hi[:, i * HALF : i * HALF + rest]], axis=1)
        for i in range(3)
    ]

    dx_own, dx_far = [dot(summed, w, ((1,), (1,))).astype(BF) for w in (own_gu, far_gu)]
    dx = jnp.stack([jnp.where(yh == 0, dx_own, dx_far), jnp.where(yh == 0, dx_far, dx_own)])
    dx = dx.reshape(2, 2, rows, 2, WPART).transpose(1, 0, 3, 2, 4).reshape(8, rows, WPART)
    dx = jnp.sum(lax.all_to_all(dx, COLUMN, 0, 0).astype(F32), axis=0)
    dx_hi = dx.astype(BF)
    dx_lo = (dx - dx_hi.astype(F32)).astype(BF)
    token_grad = dot(dx_hi, spread, ((1,), (1,))) + dot(dx_lo, spread, ((1,), (1,)))

    pg = [dot(perm_p, in_p[h], ((1,), (0,))).astype(BF) for h in range(2)]
    pg = jnp.stack(
        [
            jnp.concatenate([pg[0][:, c * HALF : (c + 1) * HALF], pg[1][:, c * HALF : c * HALF + rest]], axis=1)
            for c in range(2)
        ],
        axis=1,
    ).reshape(local_e, er, 2, part)
    low_back = lax.dot_general(
        pg, delta_out, (((2, 3), (2, 3)), ((0,), (0,))), preferred_element_type=F32
    )
    low_grad = width_sum(low_back, mask)
    grad_delta_out = lax.dot_general(
        low, pg, (((1,), (1,)), ((0,), (0,))), preferred_element_type=F32
    ).astype(BF)
    grad_delta_in = bdot(rows_x, low_grad, ((1,), (1,))).astype(BF)
    back = bdot(low_grad, delta_in, ((2,), (2,))).astype(BF).reshape(slots, part)
    back = dot(perm_x, back, ((0,), (0,))).astype(BF).reshape(n_exp, XROWS, part)
    back = lax.all_to_all(back, EXPERT, 0, 0).reshape(n_exp * XROWS, part)
    grad_tokens = (token_grad + dot(picker, back, ((0,), (0,)))).astype(BF)
    return (grad_tokens, grads[0], grads[1], grads[2].T, grad_delta_in, grad_delta_out)


def solution(mesh):
    fine = Mesh(mesh.devices.reshape(2, 4, 4, 2, 2), ("yh", "z", "x", "yl", "c"))
    return jax.shard_map(
        local,
        mesh=fine,
        in_specs=(
            P(EXPERT, WIDTH),
            P(EXPERT, WIDTH),
            P(EXPERT, None),
            P(EXPERT, None),
            P(EXPERT),
            P(EXPERT, WIDTH),
            P(EXPERT, WIDTH),
            P(WIDTH, EXPERT),
            P(EXPERT, WIDTH, None),
            P(EXPERT, None, None, WIDTH),
        ),
        out_specs=(
            P(EXPERT, WIDTH),
            P(EXPERT, WIDTH),
            P(EXPERT, WIDTH),
            P(WIDTH, EXPERT),
            P(EXPERT, WIDTH, None),
            P(EXPERT, None, None, WIDTH),
        ),
        check_vma=False,
    )
```

```python
import jax
import jax.numpy as jnp
from jax import lax
from jax.sharding import Mesh, PartitionSpec as P

BF = jnp.bfloat16
F32 = jnp.float32
EXPERT = ("yh", "z", "x")
PLANE = ("z", "x")
WIDTH = ("yl", "c")
COLUMN = ("yh", "yl", "c")
CAP = 5
HALF = 384
PADDED = 96
WPART = 768
XROWS = 24


def dot(a, b, dims):
    return lax.dot_general(a, b, (dims, ((), ())), preferred_element_type=F32)


def bdot(a, b, dims):
    return lax.dot_general(a, b, (dims, ((0,), (0,))), preferred_element_type=F32)


def targets_of(routes_t, experts):
    flat = routes_t.reshape(1, -1)
    pairs = flat.shape[1]
    onehot = (flat == lax.broadcasted_iota(jnp.int32, (experts, pairs), 0)).astype(BF)
    earlier = lax.broadcasted_iota(jnp.int32, (pairs, pairs), 0) < lax.broadcasted_iota(
        jnp.int32, (pairs, pairs), 1
    )
    before = dot(onehot, earlier.astype(BF), ((1,), (0,)))
    place = jnp.sum(before * onehot.astype(F32), axis=0).astype(jnp.int32)
    return place.reshape(routes_t.shape)


def width_sum(partial, mask):
    parts = lax.all_to_all(partial.astype(BF), WIDTH, 0, 0)
    total = jnp.sum(parts.astype(F32), axis=0)
    mine = (total * mask).astype(BF)
    return lax.all_gather(mine, WIDTH)


def pad_cols(a):
    return jnp.pad(a, ((0, 0),) * (a.ndim - 1) + ((0, 2 * HALF - a.shape[-1]),))


def swap_y(a):
    return lax.ppermute(a, "yh", [(0, 1), (1, 0)])


def after(value, first):
    return lax.optimization_barrier((value, first))[0]


def ring_send(v, axis, dim):
    at = lax.axis_index(axis)

    def entry(k):
        return lax.dynamic_index_in_dim(v, (at + k) % 4, dim, keepdims=False)

    return [entry(0)] + [lax.ppermute(entry(k), axis, [(i, (i + k) % 4) for i in range(4)]) for k in (1, 3, 2)]


def ring_total(parts, first):
    parts = after(parts, first)
    return sum((p.astype(F32) for p in parts[1:]), parts[0].astype(F32)).astype(BF)


def local(tokens, grad_out, routes, gates, ranks, w_gate, w_up, w_down, delta_in, delta_out):
    yh = lax.axis_index("yh")
    wi = lax.axis_index("yl") * 2 + lax.axis_index("c")
    rows, part = tokens.shape
    local_e, _, rank_max = delta_in.shape
    n_exp = 32
    experts = n_exp * local_e
    slots = experts * CAP
    er = n_exp * CAP
    wr = w_gate.shape[0]
    rest = part - HALF

    d_id = lax.broadcasted_iota(jnp.int32, (part, WPART), 0)
    j_id = lax.broadcasted_iota(jnp.int32, (part, WPART), 1)
    spread = ((d_id // wr == j_id // PADDED) & (d_id % wr == j_id % PADDED)).astype(BF)

    w3 = jnp.stack([pad_cols(w_gate), pad_cols(w_up), pad_cols(w_down.T)], axis=1)
    w3 = jnp.pad(w3, ((0, PADDED - wr), (0, 0), (0, 0)))
    keep = lax.dynamic_slice_in_dim(w3, yh * HALF, HALF, 2).reshape(PADDED, 3 * HALF)
    give = lax.dynamic_slice_in_dim(w3, (1 - yh) * HALF, HALF, 2).reshape(PADDED, 3 * HALF)
    both_w = lax.all_gather(jnp.stack([keep, swap_y(give)]), PLANE)
    own_w, far_w = [both_w[:, i].reshape(2 * WPART, 3 * HALF) for i in range(2)]

    place = targets_of(routes.T, experts)
    routes_t, gates_t = routes.T, gates.T
    info = jnp.concatenate([(routes_t * 8 + place).astype(F32), gates_t], axis=0)
    far = swap_y(info)
    info2 = jnp.where(
        yh == 0, jnp.concatenate([info, far], axis=1), jnp.concatenate([far, info], axis=1)
    )
    target = (routes_t // local_e) * XROWS + (routes_t % local_e) * CAP + place
    slot_ids = lax.broadcasted_iota(jnp.int32, (n_exp * XROWS, rows), 0)
    picker = sum((target[k : k + 1] == slot_ids).astype(F32) for k in range(4)).astype(BF)

    out_x = dot(picker, tokens, ((1,), (0,))).astype(BF).reshape(n_exp, XROWS, part)
    in_x = lax.all_to_all(out_x, EXPERT, 0, 0).reshape(n_exp * XROWS, part)

    xy = jnp.stack([dot(tokens, spread, ((1,), (0,))), dot(grad_out, spread, ((1,), (0,)))]).astype(BF)
    xy = lax.all_gather(xy, COLUMN).reshape(2, 4, 2, rows, WPART)

    def feats(first, which):
        two = lax.dynamic_slice_in_dim(xy[:, :, which], first, 2, 1)
        return two.transpose(0, 2, 1, 3).reshape(2 * rows, 2 * WPART)

    own_x, far_x, own_y, far_y = [feats(f, k) for k in (0, 1) for f in (2 * yh, 2 - 2 * yh)]

    def order(width, source):
        r = lax.broadcasted_iota(jnp.int32, (slots, width), 0)
        s_in = lax.broadcasted_iota(jnp.int32, (slots, width), 1)
        return (s_in == source(r // er, (r % er) // (2 * CAP), (r % (2 * CAP)) // CAP, r % CAP)).astype(BF)

    perm_x = order(n_exp * XROWS, lambda e, zx, b, p: (b * 16 + zx) * XROWS + e * CAP + p)
    perm_p = order(slots, lambda e, zx, b, p: (zx * 2 + b) * (local_e * CAP) + e * CAP + p)
    rows_x = dot(perm_x, in_x, ((1,), (0,))).astype(BF).reshape(local_e, er, part)
    rank_ids = lax.broadcasted_iota(jnp.int32, (1, rank_max), 1)
    mask = (rank_ids < ranks[wi]).astype(F32)
    low = width_sum(bdot(rows_x, delta_in, ((2,), (1,))), mask)
    halves = []
    for h in range(2):
        cols = []
        for c in range(2):
            d = bdot(low, delta_out[:, :, c, h * HALF : min(part, (h + 1) * HALF)], ((2,), (1,)))
            d = d.astype(BF)
            if h == 1:
                d = jnp.pad(d, ((0, 0), (0, 0), (0, 2 * HALF - part)))
            cols.append(d)
        cols = jnp.concatenate(cols, axis=2).reshape(slots, 2 * HALF)
        halves.append(dot(perm_p, cols, ((0,), (0,))).astype(BF).reshape(16, 2 * local_e * CAP, 2 * HALF))
    back_pre = lax.all_to_all(jnp.concatenate(halves, axis=0), EXPERT, 0, 0)
    back_pre = back_pre.reshape(2 * slots, 2 * HALF)

    coded = info2[:4].astype(jnp.int32)
    route2, place2 = coded // 8, coded % 8
    block2 = lax.broadcasted_iota(jnp.int32, (4, 2 * rows), 1) // rows
    target2 = ((route2 // local_e) * 2 + block2) * (local_e * CAP) + (route2 % local_e) * CAP + place2
    ids2 = lax.broadcasted_iota(jnp.int32, (2 * slots, 2 * rows), 0)
    hits = [target2[k : k + 1] == ids2 for k in range(4)]
    picker2 = sum(h.astype(F32) for h in hits).astype(BF)
    gate_slot = jnp.sum(
        sum(jnp.where(h, info2[4 + k : 5 + k], 0.0) for k, h in enumerate(hits)), axis=1, keepdims=True
    )

    own_gu, own_d, far_gu, far_d = own_w[:, : 2 * HALF], own_w[:, 2 * HALF :], far_w[:, : 2 * HALF], far_w[:, 2 * HALF :]
    base = (dot(own_x, own_gu, ((1,), (0,))) + dot(far_x, far_gu, ((1,), (0,)))).astype(BF)
    down = (dot(own_y, own_d, ((1,), (0,))) + dot(far_y, far_d, ((1,), (0,)))).astype(BF)
    pre = dot(picker2, base, ((1,), (0,))) + back_pre.astype(F32)
    pair_down = (gate_slot * dot(picker2, down, ((1,), (0,)))).astype(BF).astype(F32)
    act, up = pre[:, :HALF], pre[:, HALF:]
    sig = jax.nn.sigmoid(act)
    swish = act * sig
    weighted = (gate_slot * (swish * up)).astype(BF)
    grad_act = pair_down * up * sig * (1.0 + act * (1.0 - sig))
    grad_up_ = pair_down * swish
    pair_grad = jnp.concatenate([grad_act, grad_up_], axis=1).astype(BF)
    in_p = lax.all_to_all(pair_grad.reshape(n_exp, 2 * local_e * CAP, 2 * HALF), EXPERT, 0, 0)
    in_p = in_p.reshape(2, slots, 2 * HALF)
    mixed = dot(picker2, weighted, ((0,), (0,))).astype(BF)
    summed = dot(picker2, pair_grad, ((0,), (0,))).astype(BF)

    def plane_send(feat, grad, axis):
        dw = dot(feat, grad, ((0,), (0,))).astype(BF).reshape(4, 4, PADDED, -1)
        return ring_send(dw, axis, 1 if axis == "x" else 0)

    way = ("x", "z", "z", "x")
    turn = {"x": "z", "z": "x"}
    flying = [
        plane_send(f, g, a)
        for f, g, a in zip((far_x, far_y, own_x, own_y), (summed, mixed, summed, mixed), way)
    ]

    core, low_y = lax.axis_index("c"), lax.axis_index("yl")

    def dx_part(w, at):
        w_at = lax.dynamic_slice_in_dim(w, at * WPART, WPART, 0)[:, : 2 * HALF]
        return dot(summed, w_at, ((1,), (1,))).astype(BF)

    swap = [(0, 1), (1, 0)]
    dx_core = [(dx_part(w, core), lax.ppermute(dx_part(w, 1 - core), "c", swap)) for w in (own_w, far_w)]

    pg = [dot(perm_p, in_p[h], ((1,), (0,))).astype(BF) for h in range(2)]
    pg = jnp.stack(
        [
            jnp.concatenate([pg[0][:, c * HALF : (c + 1) * HALF], pg[1][:, c * HALF : c * HALF + rest]], axis=1)
            for c in range(2)
        ],
        axis=1,
    ).reshape(local_e, er, 2, part)
    low_back = lax.dot_general(
        pg, delta_out, (((2, 3), (2, 3)), ((0,), (0,))), preferred_element_type=F32
    )
    low_grad = width_sum(low_back, mask)
    flying = [ring_send(ring_total(v, low_back), turn[a], 0) for v, a in zip(flying, way)]
    dx_core = after(dx_core, low_back)
    dx_own, dx_far = [(m.astype(F32) + g.astype(F32)).astype(BF) for m, g in dx_core]
    at_own = low_y == yh
    dx_keep, dx_give = jnp.where(at_own, dx_own, dx_far), jnp.where(at_own, dx_far, dx_own)
    dx_got = lax.ppermute(dx_give, "yl", swap)
    grad_delta_out = lax.dot_general(
        low, pg, (((1,), (1,)), ((0,), (0,))), preferred_element_type=F32
    ).astype(BF)
    grad_delta_in = bdot(rows_x, low_grad, ((1,), (1,))).astype(BF)
    back = bdot(low_grad, delta_in, ((2,), (2,))).astype(BF).reshape(slots, part)
    back = dot(perm_x, back, ((0,), (0,))).astype(BF).reshape(n_exp, XROWS, part)
    dx_keep, dx_got = after((dx_keep, dx_got), back)
    dx = (dx_keep.astype(F32) + dx_got.astype(F32)).astype(BF)
    dx_keep = lax.dynamic_slice_in_dim(dx, yh * rows, rows, 0)
    dx_give = lax.dynamic_slice_in_dim(dx, (1 - yh) * rows, rows, 0)
    dx = dx_keep.astype(F32) + swap_y(dx_give).astype(F32)
    dx_hi = dx.astype(BF)
    dx_lo = (dx - dx_hi.astype(F32)).astype(BF)
    token_grad = dot(dx_hi, spread, ((1,), (1,))) + dot(dx_lo, spread, ((1,), (1,)))

    other_x, other_y, mine_x, mine_y = [ring_total(v, back) for v in flying]
    other = swap_y(jnp.concatenate([other_x, other_y], axis=1))
    mine = jnp.concatenate([mine_x, mine_y], axis=1)
    lo = jnp.where(yh == 0, mine, other)[:wr]
    hi = jnp.where(yh == 0, other, mine)[:wr]
    grads = [
        jnp.concatenate([lo[:, i * HALF : (i + 1) * HALF], hi[:, i * HALF : i * HALF + rest]], axis=1)
        for i in range(3)
    ]
    back = lax.all_to_all(back, EXPERT, 0, 0).reshape(n_exp * XROWS, part)
    grad_tokens = (token_grad + dot(picker, back, ((0,), (0,)))).astype(BF)
    return (grad_tokens, grads[0], grads[1], grads[2].T, grad_delta_in, grad_delta_out)


def solution(mesh):
    fine = Mesh(mesh.devices.reshape(2, 4, 4, 2, 2), ("yh", "z", "x", "yl", "c"))
    return jax.shard_map(
        local,
        mesh=fine,
        in_specs=(
            P(EXPERT, WIDTH),
            P(EXPERT, WIDTH),
            P(EXPERT, None),
            P(EXPERT, None),
            P(EXPERT),
            P(EXPERT, WIDTH),
            P(EXPERT, WIDTH),
            P(WIDTH, EXPERT),
            P(EXPERT, WIDTH, None),
            P(EXPERT, None, None, WIDTH),
        ),
        out_specs=(
            P(EXPERT, WIDTH),
            P(EXPERT, WIDTH),
            P(EXPERT, WIDTH),
            P(WIDTH, EXPERT),
            P(EXPERT, WIDTH, None),
            P(EXPERT, None, None, WIDTH),
        ),
        check_vma=False,
    )
```

```python
import jax
import jax.numpy as jnp
from jax import lax
from jax.experimental import pallas as pl
from jax.experimental.pallas import tpu as pltpu
from jax.sharding import Mesh, PartitionSpec as P

BF = jnp.bfloat16
F32 = jnp.float32
EXPERT = ("yh", "z", "x")
PLANE = ("z", "x")
WIDTH = ("yl", "c")
COLUMN = ("yh", "yl", "c")
CAP = 5
HALF = 384
PADDED = 96
WPART = 768
XROWS = 24


def dot(a, b, dims):
    return lax.dot_general(a, b, (dims, ((), ())), preferred_element_type=F32)


def bdot(a, b, dims):
    return lax.dot_general(a, b, (dims, ((0,), (0,))), preferred_element_type=F32)


def targets_of(routes_t, experts):
    flat = routes_t.reshape(1, -1)
    pairs = flat.shape[1]
    onehot = (flat == lax.broadcasted_iota(jnp.int32, (experts, pairs), 0)).astype(BF)
    earlier = lax.broadcasted_iota(jnp.int32, (pairs, pairs), 0) < lax.broadcasted_iota(
        jnp.int32, (pairs, pairs), 1
    )
    before = dot(onehot, earlier.astype(BF), ((1,), (0,)))
    place = jnp.sum(before * onehot.astype(F32), axis=0).astype(jnp.int32)
    return place.reshape(routes_t.shape)


def width_sum(partial, mask):
    parts = lax.all_to_all(partial.astype(BF), WIDTH, 0, 0)
    total = jnp.sum(parts.astype(F32), axis=0)
    mine = (total * mask).astype(BF)
    return lax.all_gather(mine, WIDTH)


def pad_cols(a):
    return jnp.pad(a, ((0, 0),) * (a.ndim - 1) + ((0, 2 * HALF - a.shape[-1]),))


def swap_y(a):
    return lax.ppermute(a, "yh", [(0, 1), (1, 0)])


def pair_kernel(target, gates, base, down, back, pg_out, mixed_out, summed_out, mixed_acc, summed_acc):
    step = pl.program_id(0)
    tile, tokens = back.shape[0], base.shape[0]
    ids = lax.broadcasted_iota(jnp.int32, (tile, tokens), 0) + step * tile
    pick = jnp.zeros((tile, tokens), F32)
    gate = jnp.zeros((tile, tokens), F32)
    for k in range(4):
        hit = target[k : k + 1, :] == ids
        pick = jnp.where(hit, 1.0, pick)
        gate = jnp.where(hit, gates[k : k + 1, :], gate)
    gate = jnp.sum(gate, axis=1, keepdims=True)
    pick = pick.astype(BF)
    pre = dot(pick, base[...], ((1,), (0,))) + back[...].astype(F32)
    pair_down = (gate * dot(pick, down[...], ((1,), (0,)))).astype(BF).astype(F32)
    act, up = pre[:, :HALF], pre[:, HALF:]
    sig = jax.nn.sigmoid(act)
    swish = act * sig
    weighted = (gate * (swish * up)).astype(BF)
    grad_act = (pair_down * up * sig * (1.0 + act * (1.0 - sig))).astype(BF)
    grad_up = (pair_down * swish).astype(BF)
    pg_out[:, :HALF] = grad_act
    pg_out[:, HALF:] = grad_up

    @pl.when(step == 0)
    def _():
        mixed_acc[...] = jnp.zeros_like(mixed_acc)
        summed_acc[...] = jnp.zeros_like(summed_acc)

    mixed_acc[...] += dot(pick, weighted, ((0,), (0,)))
    summed_acc[:, :HALF] += dot(pick, grad_act, ((0,), (0,)))
    summed_acc[:, HALF:] += dot(pick, grad_up, ((0,), (0,)))

    @pl.when(step == pl.num_programs(0) - 1)
    def _():
        mixed_out[...] = mixed_acc[...].astype(BF)
        summed_out[...] = summed_acc[...].astype(BF)


def pair_step(target, gates, base, down, back):
    slots, tokens, tile = back.shape[0], base.shape[0], 320

    def whole(a):
        return pl.BlockSpec(a.shape, lambda i: (0, 0))

    tiled = pl.BlockSpec((tile, 2 * HALF), lambda i: (i, 0))
    sums = [pl.BlockSpec((tokens, n * HALF), lambda i: (0, 0)) for n in (1, 2)]
    return pl.pallas_call(
        pair_kernel,
        grid=(slots // tile,),
        in_specs=[whole(target), whole(gates), whole(base), whole(down), tiled],
        out_specs=[tiled] + sums,
        out_shape=[
            jax.ShapeDtypeStruct((slots, 2 * HALF), BF),
            jax.ShapeDtypeStruct((tokens, HALF), BF),
            jax.ShapeDtypeStruct((tokens, 2 * HALF), BF),
        ],
        scratch_shapes=[pltpu.VMEM((tokens, HALF), F32), pltpu.VMEM((tokens, 2 * HALF), F32)],
        compiler_params=pltpu.CompilerParams(vmem_limit_bytes=40 * 2**20),
        cost_estimate=pl.CostEstimate(
            flops=4 * slots * tokens * 3 * HALF, bytes_accessed=5 * 2**20, transcendentals=slots * HALF
        ),
    )(target, gates, base, down, back)


def after(value, first):
    return lax.optimization_barrier((value, first))[0]


def ring_send(vs, axis, dim):
    at = lax.axis_index(axis)

    def entry(k):
        return jnp.concatenate(
            [lax.dynamic_index_in_dim(v, (at + k) % 4, dim, keepdims=False) for v in vs], axis=-1
        )

    return [entry(0)] + [lax.ppermute(entry(k), axis, [(i, (i + k) % 4) for i in range(4)]) for k in (1, 3, 2)]


def ring_total(parts, first):
    parts = after(parts, first)
    return sum((p.astype(F32) for p in parts[1:]), parts[0].astype(F32)).astype(BF)


def local(tokens, grad_out, routes, gates, ranks, w_gate, w_up, w_down, delta_in, delta_out):
    yh = lax.axis_index("yh")
    wi = lax.axis_index("yl") * 2 + lax.axis_index("c")
    rows, part = tokens.shape
    local_e, _, rank_max = delta_in.shape
    n_exp = 32
    experts = n_exp * local_e
    slots = experts * CAP
    er = n_exp * CAP
    wr = w_gate.shape[0]
    rest = part - HALF

    d_id = lax.broadcasted_iota(jnp.int32, (part, WPART), 0)
    j_id = lax.broadcasted_iota(jnp.int32, (part, WPART), 1)
    spread = ((d_id // wr == j_id // PADDED) & (d_id % wr == j_id % PADDED)).astype(BF)

    place = targets_of(routes.T, experts)
    routes_t, gates_t = routes.T, gates.T
    info = jnp.concatenate([(routes_t * 8 + place).astype(F32), gates_t], axis=0)
    target = (routes_t // local_e) * XROWS + (routes_t % local_e) * CAP + place
    slot_ids = lax.broadcasted_iota(jnp.int32, (n_exp * XROWS, rows), 0)
    picker = sum((target[k : k + 1] == slot_ids).astype(F32) for k in range(4)).astype(BF)

    out_x = dot(picker, tokens, ((1,), (0,))).astype(BF).reshape(n_exp, XROWS, part)
    in_x = lax.all_to_all(out_x, EXPERT, 0, 0).reshape(n_exp * XROWS, part)

    xy = jnp.stack([dot(tokens, spread, ((1,), (0,))), dot(grad_out, spread, ((1,), (0,)))]).astype(BF)
    xy = lax.all_gather(xy, COLUMN).reshape(2, 4, 2, rows, WPART)

    def feats(first, which):
        two = lax.dynamic_slice_in_dim(xy[:, :, which], first, 2, 1)
        return two.transpose(0, 2, 1, 3).reshape(2 * rows, 2 * WPART)

    own_x, far_x, own_y, far_y = [feats(f, k) for k in (0, 1) for f in (2 * yh, 2 - 2 * yh)]

    far = swap_y(after(info, out_x))
    info2 = jnp.where(
        yh == 0, jnp.concatenate([info, far], axis=1), jnp.concatenate([far, info], axis=1)
    )

    w3 = jnp.stack([pad_cols(w_gate), pad_cols(w_up), pad_cols(w_down.T)], axis=1)
    w3 = jnp.pad(w3, ((0, PADDED - wr), (0, 0), (0, 0)))
    keep = lax.dynamic_slice_in_dim(w3, yh * HALF, HALF, 2).reshape(PADDED, 3 * HALF)
    give = lax.dynamic_slice_in_dim(w3, (1 - yh) * HALF, HALF, 2).reshape(PADDED, 3 * HALF)
    both_w = lax.all_gather(after(jnp.stack([keep, swap_y(give)]), out_x), PLANE)
    own_w, far_w = [both_w[:, i].reshape(2 * WPART, 3 * HALF) for i in range(2)]

    def order(width, source):
        r = lax.broadcasted_iota(jnp.int32, (slots, width), 0)
        s_in = lax.broadcasted_iota(jnp.int32, (slots, width), 1)
        return (s_in == source(r // er, (r % er) // (2 * CAP), (r % (2 * CAP)) // CAP, r % CAP)).astype(BF)

    perm_x = order(n_exp * XROWS, lambda e, zx, b, p: (b * 16 + zx) * XROWS + e * CAP + p)
    perm_p = order(slots, lambda e, zx, b, p: (zx * 2 + b) * (local_e * CAP) + e * CAP + p)
    rows_x = dot(perm_x, in_x, ((1,), (0,))).astype(BF).reshape(local_e, er, part)
    rank_ids = lax.broadcasted_iota(jnp.int32, (1, rank_max), 1)
    mask = (rank_ids < ranks[wi]).astype(F32)
    low = width_sum(bdot(rows_x, delta_in, ((2,), (1,))), mask)
    halves = []
    for h in range(2):
        cols = []
        for c in range(2):
            d = bdot(low, delta_out[:, :, c, h * HALF : min(part, (h + 1) * HALF)], ((2,), (1,)))
            d = d.astype(BF)
            if h == 1:
                d = jnp.pad(d, ((0, 0), (0, 0), (0, 2 * HALF - part)))
            cols.append(d)
        cols = jnp.concatenate(cols, axis=2).reshape(slots, 2 * HALF)
        halves.append(dot(perm_p, cols, ((0,), (0,))).astype(BF).reshape(16, 2 * local_e * CAP, 2 * HALF))
    back_pre = lax.all_to_all(jnp.concatenate(halves, axis=0), EXPERT, 0, 0)
    back_pre = back_pre.reshape(2 * slots, 2 * HALF)

    coded = info2[:4].astype(jnp.int32)
    route2, place2 = coded // 8, coded % 8
    block2 = lax.broadcasted_iota(jnp.int32, (4, 2 * rows), 1) // rows
    target2 = ((route2 // local_e) * 2 + block2) * (local_e * CAP) + (route2 % local_e) * CAP + place2

    own_gu, own_d, far_gu, far_d = own_w[:, : 2 * HALF], own_w[:, 2 * HALF :], far_w[:, : 2 * HALF], far_w[:, 2 * HALF :]
    base = (dot(own_x, own_gu, ((1,), (0,))) + dot(far_x, far_gu, ((1,), (0,)))).astype(BF)
    down = (dot(own_y, own_d, ((1,), (0,))) + dot(far_y, far_d, ((1,), (0,)))).astype(BF)
    pair_grad, mixed, summed = pair_step(target2, info2[4:], base, down, back_pre)
    in_p = lax.all_to_all(pair_grad.reshape(n_exp, 2 * local_e * CAP, 2 * HALF), EXPERT, 0, 0)
    in_p = in_p.reshape(2, slots, 2 * HALF)

    def plane_send(feats, axis, first=None):
        dws = [
            dot(f, g, ((0,), (0,))).astype(BF).reshape(4, 4, PADDED, -1) for f, g in zip(feats, (summed, mixed))
        ]
        if first is not None:
            dws = after(dws, first)
        return ring_send(dws, axis, 1 if axis == "x" else 0)

    far_parts = plane_send((far_x, far_y), "x")

    pg = [dot(perm_p, in_p[h], ((1,), (0,))).astype(BF) for h in range(2)]
    pg = jnp.stack(
        [
            jnp.concatenate([pg[0][:, c * HALF : (c + 1) * HALF], pg[1][:, c * HALF : c * HALF + rest]], axis=1)
            for c in range(2)
        ],
        axis=1,
    ).reshape(local_e, er, 2, part)
    low_back = lax.dot_general(
        pg, delta_out, (((2, 3), (2, 3)), ((0,), (0,))), preferred_element_type=F32
    )
    own_parts = plane_send((own_x, own_y), "z", low_back)
    low_grad = width_sum(low_back, mask)
    grad_delta_out = lax.dot_general(
        low, pg, (((1,), (1,)), ((0,), (0,))), preferred_element_type=F32
    ).astype(BF)
    grad_delta_in = bdot(rows_x, low_grad, ((1,), (1,))).astype(BF)
    back = bdot(low_grad, delta_in, ((2,), (2,))).astype(BF).reshape(slots, part)
    back = dot(perm_x, back, ((0,), (0,))).astype(BF).reshape(n_exp, XROWS, part)
    summed_late = after(summed, low_back)
    core, low_y = lax.axis_index("c"), lax.axis_index("yl")

    def dx_part(w, at):
        w_at = lax.dynamic_slice_in_dim(w, at * WPART, WPART, 0)[:, : 2 * HALF]
        return dot(summed_late, w_at, ((1,), (1,))).astype(BF)

    swap = [(0, 1), (1, 0)]
    dx_core = (
        jnp.stack([dx_part(w, core) for w in (own_w, far_w)]),
        lax.ppermute(jnp.stack([dx_part(w, 1 - core) for w in (own_w, far_w)]), "c", swap),
    )
    far_parts = ring_send([ring_total(far_parts, back)], "z", 0)
    own_parts = ring_send([ring_total(own_parts, back)], "x", 0)
    dx_core = after(dx_core, back)
    dx_own, dx_far = [(dx_core[0][i].astype(F32) + dx_core[1][i].astype(F32)).astype(BF) for i in range(2)]
    at_own = low_y == yh
    dx_keep, dx_give = jnp.where(at_own, dx_own, dx_far), jnp.where(at_own, dx_far, dx_own)
    dx_got = lax.ppermute(dx_give, "yl", swap)
    dx = (dx_keep.astype(F32) + dx_got.astype(F32)).astype(BF)
    dx_keep = lax.dynamic_slice_in_dim(dx, yh * rows, rows, 0)
    dx_give = lax.dynamic_slice_in_dim(dx, (1 - yh) * rows, rows, 0)
    dx = dx_keep.astype(F32) + swap_y(dx_give).astype(F32)
    dx_hi = dx.astype(BF)
    dx_lo = (dx - dx_hi.astype(F32)).astype(BF)
    token_grad = dot(dx_hi, spread, ((1,), (1,))) + dot(dx_lo, spread, ((1,), (1,)))

    other = swap_y(ring_total(far_parts, back))
    mine = ring_total(own_parts, back)
    lo = jnp.where(yh == 0, mine, other)[:wr]
    hi = jnp.where(yh == 0, other, mine)[:wr]
    grads = [
        jnp.concatenate([lo[:, i * HALF : (i + 1) * HALF], hi[:, i * HALF : i * HALF + rest]], axis=1)
        for i in range(3)
    ]
    back = lax.all_to_all(back, EXPERT, 0, 0).reshape(n_exp * XROWS, part)
    grad_tokens = (token_grad + dot(picker, back, ((0,), (0,)))).astype(BF)
    return (grad_tokens, grads[0], grads[1], grads[2].T, grad_delta_in, grad_delta_out)


def solution(mesh):
    fine = Mesh(mesh.devices.reshape(2, 4, 4, 2, 2), ("yh", "z", "x", "yl", "c"))
    return jax.shard_map(
        local,
        mesh=fine,
        in_specs=(
            P(EXPERT, WIDTH),
            P(EXPERT, WIDTH),
            P(EXPERT, None),
            P(EXPERT, None),
            P(EXPERT),
            P(EXPERT, WIDTH),
            P(EXPERT, WIDTH),
            P(WIDTH, EXPERT),
            P(EXPERT, WIDTH, None),
            P(EXPERT, None, None, WIDTH),
        ),
        out_specs=(
            P(EXPERT, WIDTH),
            P(EXPERT, WIDTH),
            P(EXPERT, WIDTH),
            P(WIDTH, EXPERT),
            P(EXPERT, WIDTH, None),
            P(EXPERT, None, None, WIDTH),
        ),
        check_vma=False,
    )
```

```python
import jax
import jax.numpy as jnp
from jax import lax
from jax.experimental import pallas as pl
from jax.experimental.pallas import tpu as pltpu
from jax.sharding import Mesh, PartitionSpec as P

BF = jnp.bfloat16
F32 = jnp.float32
EXPERT = ("yh", "z", "x")
PLANE = ("z", "x")
WIDTH = ("yl", "c")
CAP = 5
HALF = 384
PADDED = 96
WPART = 768
XROWS = 24


def dot(a, b, dims):
    return lax.dot_general(a, b, (dims, ((), ())), preferred_element_type=F32)


def bdot(a, b, dims):
    return lax.dot_general(a, b, (dims, ((0,), (0,))), preferred_element_type=F32)


def targets_of(routes_t, experts):
    flat = routes_t.reshape(1, -1)
    pairs = flat.shape[1]
    onehot = (flat == lax.broadcasted_iota(jnp.int32, (experts, pairs), 0)).astype(BF)
    earlier = lax.broadcasted_iota(jnp.int32, (pairs, pairs), 0) < lax.broadcasted_iota(
        jnp.int32, (pairs, pairs), 1
    )
    before = dot(onehot, earlier.astype(BF), ((1,), (0,)))
    place = jnp.sum(before * onehot.astype(F32), axis=0).astype(jnp.int32)
    return place.reshape(routes_t.shape)


def width_sum(partial, mask):
    parts = lax.all_to_all(partial.astype(BF), WIDTH, 0, 0)
    total = jnp.sum(parts.astype(F32), axis=0)
    mine = (total * mask).astype(BF)
    return lax.all_gather(mine, WIDTH)


def pad_cols(a):
    return jnp.pad(a, ((0, 0),) * (a.ndim - 1) + ((0, 2 * HALF - a.shape[-1]),))


def swap_y(a):
    return lax.ppermute(a, "yh", [(0, 1), (1, 0)])


def pair_kernel(target, gates, base, down, back, pg_out, mixed_out, summed_out, mixed_acc, summed_acc):
    step = pl.program_id(0)
    tile, tokens = back.shape[0], base.shape[0]
    ids = lax.broadcasted_iota(jnp.int32, (tile, tokens), 0) + step * tile
    pick = jnp.zeros((tile, tokens), F32)
    gate = jnp.zeros((tile, tokens), F32)
    for k in range(4):
        hit = target[k : k + 1, :] == ids
        pick = jnp.where(hit, 1.0, pick)
        gate = jnp.where(hit, gates[k : k + 1, :], gate)
    gate = jnp.sum(gate, axis=1, keepdims=True)
    pick = pick.astype(BF)
    pre = dot(pick, base[...], ((1,), (0,))) + back[...].astype(F32)
    pair_down = (gate * dot(pick, down[...], ((1,), (0,)))).astype(BF).astype(F32)
    act, up = pre[:, :HALF], pre[:, HALF:]
    sig = jax.nn.sigmoid(act)
    swish = act * sig
    weighted = (gate * (swish * up)).astype(BF)
    grad_act = (pair_down * up * sig * (1.0 + act * (1.0 - sig))).astype(BF)
    grad_up = (pair_down * swish).astype(BF)
    pg_out[:, :HALF] = grad_act
    pg_out[:, HALF:] = grad_up

    @pl.when(step == 0)
    def _():
        mixed_acc[...] = jnp.zeros_like(mixed_acc)
        summed_acc[...] = jnp.zeros_like(summed_acc)

    mixed_acc[...] += dot(pick, weighted, ((0,), (0,)))
    summed_acc[:, :HALF] += dot(pick, grad_act, ((0,), (0,)))
    summed_acc[:, HALF:] += dot(pick, grad_up, ((0,), (0,)))

    @pl.when(step == pl.num_programs(0) - 1)
    def _():
        mixed_out[...] = mixed_acc[...].astype(BF)
        summed_out[...] = summed_acc[...].astype(BF)


def pair_step(target, gates, base, down, back):
    slots, tokens, tile = back.shape[0], base.shape[0], 320

    def whole(a):
        return pl.BlockSpec(a.shape, lambda i: (0, 0))

    tiled = pl.BlockSpec((tile, 2 * HALF), lambda i: (i, 0))
    sums = [pl.BlockSpec((tokens, n * HALF), lambda i: (0, 0)) for n in (1, 2)]
    return pl.pallas_call(
        pair_kernel,
        grid=(slots // tile,),
        in_specs=[whole(target), whole(gates), whole(base), whole(down), tiled],
        out_specs=[tiled] + sums,
        out_shape=[
            jax.ShapeDtypeStruct((slots, 2 * HALF), BF),
            jax.ShapeDtypeStruct((tokens, HALF), BF),
            jax.ShapeDtypeStruct((tokens, 2 * HALF), BF),
        ],
        scratch_shapes=[pltpu.VMEM((tokens, HALF), F32), pltpu.VMEM((tokens, 2 * HALF), F32)],
        compiler_params=pltpu.CompilerParams(vmem_limit_bytes=40 * 2**20),
        cost_estimate=pl.CostEstimate(
            flops=4 * slots * tokens * 3 * HALF, bytes_accessed=5 * 2**20, transcendentals=slots * HALF
        ),
    )(target, gates, base, down, back)


def after(value, first):
    return lax.optimization_barrier((value, first))[0]


def ring_send(vs, axis, dim, first=None):
    at = lax.axis_index(axis)

    def entry(k):
        return jnp.concatenate(
            [lax.dynamic_index_in_dim(v, (at + k) % 4, dim, keepdims=False) for v in vs], axis=-1
        )

    sent = [entry(k) for k in (1, 3, 2)]
    if first is not None:
        sent[2] = after(sent[2], first)
    return [entry(0)] + [
        lax.ppermute(v, axis, [(i, (i + k) % 4) for i in range(4)]) for v, k in zip(sent, (1, 3, 2))
    ]


def ring_total(parts, first):
    parts = after(parts, first)
    return sum((p.astype(F32) for p in parts[1:]), parts[0].astype(F32)).astype(BF)


def local(tokens, grad_out, routes, gates, ranks, w_gate, w_up, w_down, delta_in, delta_out):
    yh = lax.axis_index("yh")
    wi = lax.axis_index("yl") * 2 + lax.axis_index("c")
    rows, part = tokens.shape
    local_e, _, rank_max = delta_in.shape
    n_exp = 32
    experts = n_exp * local_e
    slots = experts * CAP
    er = n_exp * CAP
    wr = w_gate.shape[0]
    rest = part - HALF

    d_id = lax.broadcasted_iota(jnp.int32, (part, WPART), 0)
    j_id = lax.broadcasted_iota(jnp.int32, (part, WPART), 1)
    spread = ((d_id // wr == j_id // PADDED) & (d_id % wr == j_id % PADDED)).astype(BF)

    place = targets_of(routes.T, experts)
    routes_t, gates_t = routes.T, gates.T
    info = jnp.concatenate([(routes_t * 8 + place).astype(F32), gates_t], axis=0)
    target = (routes_t // local_e) * XROWS + (routes_t % local_e) * CAP + place
    slot_ids = lax.broadcasted_iota(jnp.int32, (n_exp * XROWS, rows), 0)
    picker = sum((target[k : k + 1] == slot_ids).astype(F32) for k in range(4)).astype(BF)

    out_x = dot(picker, tokens, ((1,), (0,))).astype(BF).reshape(n_exp, XROWS, part)
    in_x = lax.all_to_all(out_x, EXPERT, 0, 0).reshape(n_exp * XROWS, part)

    xy = jnp.stack([dot(tokens, spread, ((1,), (0,))), dot(grad_out, spread, ((1,), (0,)))]).astype(BF)
    core, low_y = lax.axis_index("c"), lax.axis_index("yl")
    swap = [(0, 1), (1, 0)]

    def pair_up(at, mine, theirs, axis):
        return jnp.where(
            at == 0, jnp.concatenate([mine, theirs], axis=axis), jnp.concatenate([theirs, mine], axis=axis)
        )

    near = pair_up(yh, xy, swap_y(xy), 1)
    across = lax.ppermute(near, "yl", swap)
    at_own = low_y == yh
    parts = jnp.stack([jnp.where(at_own, near, across), jnp.where(at_own, across, near)])
    parts = pair_up(core, parts, lax.ppermute(parts, "c", swap), 3)
    own_x, own_y, far_x, far_y = parts[0, 0], parts[0, 1], parts[1, 0], parts[1, 1]

    far = swap_y(after(info, out_x))
    info2 = jnp.where(
        yh == 0, jnp.concatenate([info, far], axis=1), jnp.concatenate([far, info], axis=1)
    )

    w3 = jnp.stack([pad_cols(w_gate), pad_cols(w_up), pad_cols(w_down.T)], axis=1)
    w3 = jnp.pad(w3, ((0, PADDED - wr), (0, 0), (0, 0)))
    keep = lax.dynamic_slice_in_dim(w3, yh * HALF, HALF, 2).reshape(PADDED, 3 * HALF)
    give = lax.dynamic_slice_in_dim(w3, (1 - yh) * HALF, HALF, 2).reshape(PADDED, 3 * HALF)
    both_w = lax.all_gather(after(jnp.stack([keep, swap_y(give)]), out_x), PLANE)
    own_w, far_w = [both_w[:, i].reshape(2 * WPART, 3 * HALF) for i in range(2)]

    def order(width, source):
        r = lax.broadcasted_iota(jnp.int32, (slots, width), 0)
        s_in = lax.broadcasted_iota(jnp.int32, (slots, width), 1)
        return (s_in == source(r // er, (r % er) // (2 * CAP), (r % (2 * CAP)) // CAP, r % CAP)).astype(BF)

    perm_x = order(n_exp * XROWS, lambda e, zx, b, p: (b * 16 + zx) * XROWS + e * CAP + p)
    perm_p = order(slots, lambda e, zx, b, p: (zx * 2 + b) * (local_e * CAP) + e * CAP + p)
    rows_x = dot(perm_x, in_x, ((1,), (0,))).astype(BF).reshape(local_e, er, part)
    rank_ids = lax.broadcasted_iota(jnp.int32, (1, rank_max), 1)
    mask = (rank_ids < ranks[wi]).astype(F32)
    low = width_sum(bdot(rows_x, delta_in, ((2,), (1,))), mask)
    halves = []
    for h in range(2):
        cols = []
        for c in range(2):
            d = bdot(low, delta_out[:, :, c, h * HALF : min(part, (h + 1) * HALF)], ((2,), (1,)))
            d = d.astype(BF)
            if h == 1:
                d = jnp.pad(d, ((0, 0), (0, 0), (0, 2 * HALF - part)))
            cols.append(d)
        cols = jnp.concatenate(cols, axis=2).reshape(slots, 2 * HALF)
        halves.append(dot(perm_p, cols, ((0,), (0,))).astype(BF).reshape(16, 2 * local_e * CAP, 2 * HALF))
    back_pre = lax.all_to_all(jnp.concatenate(halves, axis=0), EXPERT, 0, 0)
    back_pre = back_pre.reshape(2 * slots, 2 * HALF)

    coded = info2[:4].astype(jnp.int32)
    route2, place2 = coded // 8, coded % 8
    block2 = lax.broadcasted_iota(jnp.int32, (4, 2 * rows), 1) // rows
    target2 = ((route2 // local_e) * 2 + block2) * (local_e * CAP) + (route2 % local_e) * CAP + place2

    own_gu, own_d, far_gu, far_d = own_w[:, : 2 * HALF], own_w[:, 2 * HALF :], far_w[:, : 2 * HALF], far_w[:, 2 * HALF :]
    base = (dot(own_x, own_gu, ((1,), (0,))) + dot(far_x, far_gu, ((1,), (0,)))).astype(BF)
    down = (dot(own_y, own_d, ((1,), (0,))) + dot(far_y, far_d, ((1,), (0,)))).astype(BF)
    pair_grad, mixed, summed = pair_step(target2, info2[4:], base, down, back_pre)
    in_p = lax.all_to_all(pair_grad.reshape(n_exp, 2 * local_e * CAP, 2 * HALF), EXPERT, 0, 0)
    in_p = in_p.reshape(2, slots, 2 * HALF)

    def plane_send(feats, axis, first=None):
        dws = [
            dot(f, g, ((0,), (0,))).astype(BF).reshape(4, 4, PADDED, -1) for f, g in zip(feats, (summed, mixed))
        ]
        return ring_send(dws, axis, 1 if axis == "x" else 0, first)


    pg = [dot(perm_p, in_p[h], ((1,), (0,))).astype(BF) for h in range(2)]
    pg = jnp.stack(
        [
            jnp.concatenate([pg[0][:, c * HALF : (c + 1) * HALF], pg[1][:, c * HALF : c * HALF + rest]], axis=1)
            for c in range(2)
        ],
        axis=1,
    ).reshape(local_e, er, 2, part)
    low_back = lax.dot_general(
        pg, delta_out, (((2, 3), (2, 3)), ((0,), (0,))), preferred_element_type=F32
    )
    far_parts = plane_send((far_x, far_y), "x")
    low_back = after(low_back.astype(BF), far_parts[1])
    own_parts = plane_send((own_x, own_y), "z", low_back)
    low_grad = width_sum(low_back, mask)
    back = bdot(low_grad, delta_in, ((2,), (2,))).astype(BF).reshape(slots, part)
    grad_delta_out = lax.dot_general(
        low, after(pg, back), (((1,), (1,)), ((0,), (0,))), preferred_element_type=F32
    ).astype(BF)
    grad_delta_in = bdot(after(rows_x, back), low_grad, ((1,), (1,))).astype(BF)
    back = dot(perm_x, back, ((0,), (0,))).astype(BF).reshape(n_exp, XROWS, part)
    def dx_part(w, at):
        w_at = lax.dynamic_slice_in_dim(w, at * WPART, WPART, 0)[:, : 2 * HALF]
        return dot(summed, w_at, ((1,), (1,))).astype(BF)

    dx_core = (
        jnp.stack([dx_part(w, core) for w in (own_w, far_w)]),
        lax.ppermute(after(jnp.stack([dx_part(w, 1 - core) for w in (own_w, far_w)]), low_back), "c", swap),
    )
    far_parts = ring_send([ring_total(far_parts, back)], "z", 0)
    own_parts = ring_send([ring_total(own_parts, back)], "x", 0)
    dx_core = after(dx_core, back)
    dx_own, dx_far = [(dx_core[0][i].astype(F32) + dx_core[1][i].astype(F32)).astype(BF) for i in range(2)]
    dx_keep, dx_give = jnp.where(at_own, dx_own, dx_far), jnp.where(at_own, dx_far, dx_own)
    dx_got = lax.ppermute(dx_give, "yl", swap)
    dx = (dx_keep.astype(F32) + dx_got.astype(F32)).astype(BF)
    dx_keep = lax.dynamic_slice_in_dim(dx, yh * rows, rows, 0)
    dx_give = lax.dynamic_slice_in_dim(dx, (1 - yh) * rows, rows, 0)
    dx = dx_keep.astype(F32) + swap_y(dx_give).astype(F32)
    dx_hi = dx.astype(BF)
    dx_lo = (dx - dx_hi.astype(F32)).astype(BF)
    token_grad = dot(dx_hi, spread, ((1,), (1,))) + dot(dx_lo, spread, ((1,), (1,)))

    other = swap_y(ring_total(far_parts, back))
    mine = ring_total(own_parts, back)
    lo = jnp.where(yh == 0, mine, other)[:wr]
    hi = jnp.where(yh == 0, other, mine)[:wr]
    grads = [
        jnp.concatenate([lo[:, i * HALF : (i + 1) * HALF], hi[:, i * HALF : i * HALF + rest]], axis=1)
        for i in range(3)
    ]
    back = lax.all_to_all(back, EXPERT, 0, 0).reshape(n_exp * XROWS, part)
    grad_tokens = (token_grad + dot(picker, back, ((0,), (0,)))).astype(BF)
    return (grad_tokens, grads[0], grads[1], grads[2].T, grad_delta_in, grad_delta_out)


def solution(mesh):
    fine = Mesh(mesh.devices.reshape(2, 4, 4, 2, 2), ("yh", "z", "x", "yl", "c"))
    return jax.shard_map(
        local,
        mesh=fine,
        in_specs=(
            P(EXPERT, WIDTH),
            P(EXPERT, WIDTH),
            P(EXPERT, None),
            P(EXPERT, None),
            P(EXPERT),
            P(EXPERT, WIDTH),
            P(EXPERT, WIDTH),
            P(WIDTH, EXPERT),
            P(EXPERT, WIDTH, None),
            P(EXPERT, None, None, WIDTH),
        ),
        out_specs=(
            P(EXPERT, WIDTH),
            P(EXPERT, WIDTH),
            P(EXPERT, WIDTH),
            P(WIDTH, EXPERT),
            P(EXPERT, WIDTH, None),
            P(EXPERT, None, None, WIDTH),
        ),
        check_vma=False,
    )
```

```python
import jax
import jax.numpy as jnp
from jax import lax
from jax.experimental import pallas as pl
from jax.experimental.pallas import tpu as pltpu
from jax.sharding import Mesh, PartitionSpec as P

BF = jnp.bfloat16
F32 = jnp.float32
EXPERT = ("yh", "z", "x")
PLANE = ("z", "x")
WIDTH = ("yl", "c")
CAP = 5
HALF = 384
PADDED = 96
WPART = 768
XROWS = 24


def dot(a, b, dims):
    return lax.dot_general(a, b, (dims, ((), ())), preferred_element_type=F32)


def bdot(a, b, dims):
    return lax.dot_general(a, b, (dims, ((0,), (0,))), preferred_element_type=F32)


def targets_of(routes_t, experts):
    flat = routes_t.reshape(1, -1)
    pairs = flat.shape[1]
    onehot = (flat == lax.broadcasted_iota(jnp.int32, (experts, pairs), 0)).astype(BF)
    earlier = lax.broadcasted_iota(jnp.int32, (pairs, pairs), 0) < lax.broadcasted_iota(
        jnp.int32, (pairs, pairs), 1
    )
    before = dot(onehot, earlier.astype(BF), ((1,), (0,)))
    place = jnp.sum(before * onehot.astype(F32), axis=0).astype(jnp.int32)
    return place.reshape(routes_t.shape)


def width_sum(partial, mask):
    parts = lax.all_to_all(partial.astype(BF), WIDTH, 0, 0)
    total = jnp.sum(parts.astype(F32), axis=0)
    mine = (total * mask).astype(BF)
    return lax.all_gather(mine, WIDTH)


def pad_cols(a):
    return jnp.pad(a, ((0, 0),) * (a.ndim - 1) + ((0, 2 * HALF - a.shape[-1]),))


def swap_y(a):
    return lax.ppermute(a, "yh", [(0, 1), (1, 0)])


def pair_kernel(target, gates, base, down, back, pg_out, mixed_out, summed_out, mixed_acc, summed_acc):
    step = pl.program_id(0)
    tile, tokens = back.shape[0], base.shape[0]
    ids = lax.broadcasted_iota(jnp.int32, (tile, tokens), 0) + step * tile
    pick = jnp.zeros((tile, tokens), F32)
    gate = jnp.zeros((tile, tokens), F32)
    for k in range(4):
        hit = target[k : k + 1, :] == ids
        pick = jnp.where(hit, 1.0, pick)
        gate = jnp.where(hit, gates[k : k + 1, :], gate)
    gate = jnp.sum(gate, axis=1, keepdims=True)
    pick = pick.astype(BF)
    pre = dot(pick, base[...], ((1,), (0,))) + back[...].astype(F32)
    pair_down = (gate * dot(pick, down[...], ((1,), (0,)))).astype(BF).astype(F32)
    act, up = pre[:, :HALF], pre[:, HALF:]
    sig = jax.nn.sigmoid(act)
    swish = act * sig
    weighted = (gate * (swish * up)).astype(BF)
    grad_act = (pair_down * up * sig * (1.0 + act * (1.0 - sig))).astype(BF)
    grad_up = (pair_down * swish).astype(BF)
    pg_out[:, :HALF] = grad_act
    pg_out[:, HALF:] = grad_up

    @pl.when(step == 0)
    def _():
        mixed_acc[...] = jnp.zeros_like(mixed_acc)
        summed_acc[...] = jnp.zeros_like(summed_acc)

    mixed_acc[...] += dot(pick, weighted, ((0,), (0,)))
    summed_acc[:, :HALF] += dot(pick, grad_act, ((0,), (0,)))
    summed_acc[:, HALF:] += dot(pick, grad_up, ((0,), (0,)))

    @pl.when(step == pl.num_programs(0) - 1)
    def _():
        mixed_out[...] = mixed_acc[...].astype(BF)
        summed_out[...] = summed_acc[...].astype(BF)


def pair_step(target, gates, base, down, back):
    slots, tokens, tile = back.shape[0], base.shape[0], 320

    def whole(a):
        return pl.BlockSpec(a.shape, lambda i: (0, 0))

    tiled = pl.BlockSpec((tile, 2 * HALF), lambda i: (i, 0))
    sums = [pl.BlockSpec((tokens, n * HALF), lambda i: (0, 0)) for n in (1, 2)]
    return pl.pallas_call(
        pair_kernel,
        grid=(slots // tile,),
        in_specs=[whole(target), whole(gates), whole(base), whole(down), tiled],
        out_specs=[tiled] + sums,
        out_shape=[
            jax.ShapeDtypeStruct((slots, 2 * HALF), BF),
            jax.ShapeDtypeStruct((tokens, HALF), BF),
            jax.ShapeDtypeStruct((tokens, 2 * HALF), BF),
        ],
        scratch_shapes=[pltpu.VMEM((tokens, HALF), F32), pltpu.VMEM((tokens, 2 * HALF), F32)],
        compiler_params=pltpu.CompilerParams(vmem_limit_bytes=40 * 2**20),
        cost_estimate=pl.CostEstimate(
            flops=4 * slots * tokens * 3 * HALF, bytes_accessed=5 * 2**20, transcendentals=slots * HALF
        ),
    )(target, gates, base, down, back)


def one_expert(shape):
    return pl.BlockSpec((1,) + shape[1:], lambda e: (e,) + (0,) * (len(shape) - 1))


def all_of(shape):
    return pl.BlockSpec(shape, lambda e: (0,) * len(shape))


def expert_call(kernel, ins, outs, scratch, flops):
    def spec(shape, split):
        return one_expert(shape) if split else all_of(shape)

    return pl.pallas_call(
        kernel,
        grid=(4,),
        in_specs=[spec(a.shape, split) for a, split in ins],
        out_specs=[spec(shape, split) for shape, split in outs],
        out_shape=[jax.ShapeDtypeStruct(shape, BF) for shape, _ in outs],
        scratch_shapes=scratch,
        compiler_params=pltpu.CompilerParams(vmem_limit_bytes=40 * 2**20),
        cost_estimate=pl.CostEstimate(flops=flops, bytes_accessed=12 * 2**20, transcendentals=0),
    )(*[a for a, _ in ins])


def expert_rows(rows):
    return pl.ds(pl.multiple_of(pl.program_id(0) * rows, 32), rows)


def low_kernel(arrived, perm, factor, rows_out, low_out):
    @pl.when(pl.program_id(0) == 0)
    def _():
        rows_out[...] = dot(perm[...], arrived[...], ((1,), (0,))).astype(BF)

    mine = rows_out[expert_rows(low_out.shape[1]), :]
    low_out[0] = dot(mine, factor[0], ((1,), (0,))).astype(BF)


def pre_kernel(low, factor, perm_t, out, cols):
    step = pl.program_id(0)

    @pl.when(step == 0)
    def _():
        cols[...] = jnp.zeros_like(cols)

    rows = expert_rows(low.shape[1])
    rest = factor.shape[2] - HALF
    for c in range(2):
        pre = dot(low[0], factor[0, c], ((1,), (1,))).astype(BF)
        cols[0, rows, c * HALF : (c + 1) * HALF] = pre[:, :HALF]
        cols[1, rows, c * HALF : c * HALF + rest] = pre[:, HALF:]

    @pl.when(step == pl.num_programs(0) - 1)
    def _():
        for h in range(2):
            out[h] = dot(perm_t[...], cols[h], ((1,), (0,))).astype(BF)


def grad_kernel(arrived, perm, factor, low_out, pg_out):
    @pl.when(pl.program_id(0) == 0)
    def _():
        for h in range(2):
            both = dot(perm[...], arrived[h], ((1,), (0,))).astype(BF)
            for c in range(2):
                pg_out[c, :, h * HALF : (h + 1) * HALF] = both[:, c * HALF : (c + 1) * HALF]

    rows = expert_rows(low_out.shape[1])
    part = factor.shape[2]
    total = dot(pg_out[0, rows, :part], factor[0, 0], ((1,), (0,)))
    total += dot(pg_out[1, rows, :part], factor[0, 1], ((1,), (0,)))
    low_out[0] = total.astype(BF)


def back_kernel(low_grad, factor, perm_t, out, cols):
    step = pl.program_id(0)
    rows = expert_rows(low_grad.shape[1])
    cols[rows, :] = dot(low_grad[0], factor[0], ((1,), (1,))).astype(BF)

    @pl.when(step == pl.num_programs(0) - 1)
    def _():
        out[...] = dot(perm_t[...], cols[...], ((1,), (0,))).astype(BF)


def after(value, first):
    return lax.optimization_barrier((value, first))[0]


def hop(v, axis, k):
    return lax.ppermute(v, axis, [(i, (i + k) % 4) for i in range(4)])


def ring_send(vs, axis, dim):
    at = lax.axis_index(axis)

    def entry(k):
        return jnp.concatenate(
            [lax.dynamic_index_in_dim(v, (at + k) % 4, dim, keepdims=False) for v in vs], axis=-1
        )

    return [entry(0), hop(entry(1), axis, 1), hop(entry(3), axis, 3), entry(2)]


def ring_rest(parts, axis, first=None):
    last = parts[3] if first is None else after(parts[3], first)
    return parts[:3] + [hop(last, axis, 2)]


def ring_total(parts, first):
    parts = after(parts, first)
    return sum((p.astype(F32) for p in parts[1:]), parts[0].astype(F32)).astype(BF)


def local(tokens, grad_out, routes, gates, ranks, w_gate, w_up, w_down, delta_in, delta_out):
    yh = lax.axis_index("yh")
    wi = lax.axis_index("yl") * 2 + lax.axis_index("c")
    rows, part = tokens.shape
    local_e, _, rank_max = delta_in.shape
    n_exp = 32
    experts = n_exp * local_e
    slots = experts * CAP
    er = n_exp * CAP
    wr = w_gate.shape[0]
    rest = part - HALF

    d_id = lax.broadcasted_iota(jnp.int32, (part, WPART), 0)
    j_id = lax.broadcasted_iota(jnp.int32, (part, WPART), 1)
    spread = ((d_id // wr == j_id // PADDED) & (d_id % wr == j_id % PADDED)).astype(BF)

    place = targets_of(routes.T, experts)
    routes_t, gates_t = routes.T, gates.T
    info = jnp.concatenate([(routes_t * 8 + place).astype(F32), gates_t], axis=0)
    target = (routes_t // local_e) * XROWS + (routes_t % local_e) * CAP + place
    slot_ids = lax.broadcasted_iota(jnp.int32, (n_exp * XROWS, rows), 0)
    picker = sum((target[k : k + 1] == slot_ids).astype(F32) for k in range(4)).astype(BF)

    out_x = dot(picker, tokens, ((1,), (0,))).astype(BF).reshape(n_exp, XROWS, part)
    in_x = lax.all_to_all(out_x, EXPERT, 0, 0).reshape(n_exp * XROWS, part)

    xy = jnp.stack([dot(tokens, spread, ((1,), (0,))), dot(grad_out, spread, ((1,), (0,)))]).astype(BF)
    core, low_y = lax.axis_index("c"), lax.axis_index("yl")
    swap = [(0, 1), (1, 0)]

    def pair_up(at, mine, theirs, axis):
        return jnp.where(
            at == 0, jnp.concatenate([mine, theirs], axis=axis), jnp.concatenate([theirs, mine], axis=axis)
        )

    near = pair_up(yh, xy, swap_y(xy), 1)
    across = lax.ppermute(near, "yl", swap)
    at_own = low_y == yh
    parts = jnp.stack([jnp.where(at_own, near, across), jnp.where(at_own, across, near)])
    parts = pair_up(core, parts, lax.ppermute(parts, "c", swap), 3)
    own_x, own_y, far_x, far_y = parts[0, 0], parts[0, 1], parts[1, 0], parts[1, 1]

    far = swap_y(after(info, out_x))
    info2 = jnp.where(
        yh == 0, jnp.concatenate([info, far], axis=1), jnp.concatenate([far, info], axis=1)
    )

    w3 = jnp.stack([pad_cols(w_gate), pad_cols(w_up), pad_cols(w_down.T)], axis=1)
    w3 = jnp.pad(w3, ((0, PADDED - wr), (0, 0), (0, 0)))
    keep = lax.dynamic_slice_in_dim(w3, yh * HALF, HALF, 2).reshape(PADDED, 3 * HALF)
    give = lax.dynamic_slice_in_dim(w3, (1 - yh) * HALF, HALF, 2).reshape(PADDED, 3 * HALF)
    both_w = lax.all_gather(after(jnp.stack([keep, swap_y(give)]), out_x), PLANE)
    own_w, far_w = [both_w[:, i].reshape(2 * WPART, 3 * HALF) for i in range(2)]

    def order(width, source):
        r = lax.broadcasted_iota(jnp.int32, (slots, width), 0)
        s_in = lax.broadcasted_iota(jnp.int32, (slots, width), 1)
        return (s_in == source(r // er, (r % er) // (2 * CAP), (r % (2 * CAP)) // CAP, r % CAP)).astype(BF)

    perm_x = order(n_exp * XROWS, lambda e, zx, b, p: (b * 16 + zx) * XROWS + e * CAP + p)
    perm_p = order(slots, lambda e, zx, b, p: (zx * 2 + b) * (local_e * CAP) + e * CAP + p)
    factor_out = delta_out.transpose(0, 2, 3, 1)
    rows_x, low_part = expert_call(
        low_kernel,
        [(in_x, False), (perm_x, False), (delta_in, True)],
        [((slots, part), False), ((local_e, er, rank_max), True)],
        [],
        12 * 10**8,
    )
    rows_x = rows_x.reshape(local_e, er, part)
    rank_ids = lax.broadcasted_iota(jnp.int32, (1, rank_max), 1)
    mask = (rank_ids < ranks[wi]).astype(F32)
    low = width_sum(low_part, mask)
    [out_pre] = expert_call(
        pre_kernel,
        [(low, True), (factor_out, True), (perm_p.T, False)],
        [((2, slots, 2 * HALF), False)],
        [pltpu.VMEM((2, slots, 2 * HALF), BF)],
        22 * 10**8,
    )
    back_pre = lax.all_to_all(out_pre.reshape(n_exp, 2 * local_e * CAP, 2 * HALF), EXPERT, 0, 0)
    back_pre = back_pre.reshape(2 * slots, 2 * HALF)

    coded = info2[:4].astype(jnp.int32)
    route2, place2 = coded // 8, coded % 8
    block2 = lax.broadcasted_iota(jnp.int32, (4, 2 * rows), 1) // rows
    target2 = ((route2 // local_e) * 2 + block2) * (local_e * CAP) + (route2 % local_e) * CAP + place2

    own_gu, own_d, far_gu, far_d = own_w[:, : 2 * HALF], own_w[:, 2 * HALF :], far_w[:, : 2 * HALF], far_w[:, 2 * HALF :]
    base = (dot(own_x, own_gu, ((1,), (0,))) + dot(far_x, far_gu, ((1,), (0,)))).astype(BF)
    down = (dot(own_y, own_d, ((1,), (0,))) + dot(far_y, far_d, ((1,), (0,)))).astype(BF)
    pair_grad, mixed, summed = pair_step(target2, info2[4:], base, down, back_pre)
    in_p = lax.all_to_all(pair_grad.reshape(n_exp, 2 * local_e * CAP, 2 * HALF), EXPERT, 0, 0)
    in_p = in_p.reshape(2, slots, 2 * HALF)

    def plane_send(feats, axis):
        dws = [
            dot(f, g, ((0,), (0,))).astype(BF).reshape(4, 4, PADDED, -1) for f, g in zip(feats, (summed, mixed))
        ]
        return ring_send(dws, axis, 1 if axis == "x" else 0)

    low_back, pg = expert_call(
        grad_kernel,
        [(in_p, False), (perm_p, False), (factor_out, True)],
        [((local_e, er, rank_max), True), ((2, slots, 2 * HALF), False)],
        [],
        22 * 10**8,
    )
    far_parts = plane_send((far_x, far_y), "x")
    own_parts = plane_send((own_x, own_y), "z")
    low_back = after(low_back, (far_parts[1], far_parts[2], own_parts[1], own_parts[2]))
    far_parts, own_parts = ring_rest(far_parts, "x", low_back), ring_rest(own_parts, "z", low_back)
    low_grad = width_sum(low_back, mask)
    [back] = expert_call(
        back_kernel,
        [(low_grad, True), (delta_in, True), (perm_x.T, False)],
        [((n_exp * XROWS, part), False)],
        [pltpu.VMEM((slots, part), BF)],
        12 * 10**8,
    )
    pg = after(pg, back).reshape(2, local_e, er, 2 * HALF)[..., :part]
    grad_delta_out = lax.dot_general(
        low, pg, (((1,), (2,)), ((0,), (1,))), preferred_element_type=F32
    ).astype(BF)
    grad_delta_in = bdot(after(rows_x, back), low_grad, ((1,), (1,))).astype(BF)
    def dx_part(w, at):
        w_at = lax.dynamic_slice_in_dim(w, at * WPART, WPART, 0)[:, : 2 * HALF]
        return dot(summed, w_at, ((1,), (1,))).astype(BF)

    dx_core = (
        jnp.stack([dx_part(w, core) for w in (own_w, far_w)]),
        lax.ppermute(after(jnp.stack([dx_part(w, 1 - core) for w in (own_w, far_w)]), low_back), "c", swap),
    )
    far_parts = ring_rest(ring_send([ring_total(far_parts, back)], "z", 0), "z")
    own_parts = ring_rest(ring_send([ring_total(own_parts, back)], "x", 0), "x")
    dx_core = after(dx_core, low_grad)
    dx_own, dx_far = [(dx_core[0][i].astype(F32) + dx_core[1][i].astype(F32)).astype(BF) for i in range(2)]
    dx_keep, dx_give = jnp.where(at_own, dx_own, dx_far), jnp.where(at_own, dx_far, dx_own)
    dx_got = lax.ppermute(dx_give, "yl", swap)
    dx = (dx_keep.astype(F32) + dx_got.astype(F32)).astype(BF)
    dx_keep = lax.dynamic_slice_in_dim(dx, yh * rows, rows, 0)
    dx_give = lax.dynamic_slice_in_dim(dx, (1 - yh) * rows, rows, 0)
    dx = dx_keep.astype(F32) + swap_y(dx_give).astype(F32)
    dx_hi = dx.astype(BF)
    dx_lo = (dx - dx_hi.astype(F32)).astype(BF)
    token_grad = dot(dx_hi, spread, ((1,), (1,))) + dot(dx_lo, spread, ((1,), (1,)))

    other = swap_y(ring_total(far_parts, back))
    mine = ring_total(own_parts, back)
    lo = jnp.where(yh == 0, mine, other)[:wr]
    hi = jnp.where(yh == 0, other, mine)[:wr]
    grads = [
        jnp.concatenate([lo[:, i * HALF : (i + 1) * HALF], hi[:, i * HALF : i * HALF + rest]], axis=1)
        for i in range(3)
    ]
    back = lax.all_to_all(back.reshape(n_exp, XROWS, part), EXPERT, 0, 0).reshape(n_exp * XROWS, part)
    grad_tokens = (token_grad + dot(picker, back, ((0,), (0,)))).astype(BF)
    return (grad_tokens, grads[0], grads[1], grads[2].T, grad_delta_in, grad_delta_out)


def solution(mesh):
    fine = Mesh(mesh.devices.reshape(2, 4, 4, 2, 2), ("yh", "z", "x", "yl", "c"))
    return jax.shard_map(
        local,
        mesh=fine,
        in_specs=(
            P(EXPERT, WIDTH),
            P(EXPERT, WIDTH),
            P(EXPERT, None),
            P(EXPERT, None),
            P(EXPERT),
            P(EXPERT, WIDTH),
            P(EXPERT, WIDTH),
            P(WIDTH, EXPERT),
            P(EXPERT, WIDTH, None),
            P(EXPERT, None, None, WIDTH),
        ),
        out_specs=(
            P(EXPERT, WIDTH),
            P(EXPERT, WIDTH),
            P(EXPERT, WIDTH),
            P(WIDTH, EXPERT),
            P(EXPERT, WIDTH, None),
            P(EXPERT, None, None, WIDTH),
        ),
        check_vma=False,
    )
```

```python
import jax
import jax.numpy as jnp
from jax import lax
from jax.experimental import pallas as pl
from jax.experimental.pallas import tpu as pltpu
from jax.sharding import Mesh, PartitionSpec as P

BF = jnp.bfloat16
F32 = jnp.float32
EXPERT = ("yh", "z", "x")
PLANE = ("z", "x")
WIDTH = ("yl", "c")
CAP = 5
HALF = 384
PADDED = 96
WPART = 768
XROWS = 24


def dot(a, b, dims):
    return lax.dot_general(a, b, (dims, ((), ())), preferred_element_type=F32)


def bdot(a, b, dims):
    return lax.dot_general(a, b, (dims, ((0,), (0,))), preferred_element_type=F32)


def targets_of(routes_t, experts):
    flat = routes_t.reshape(1, -1)
    pairs = flat.shape[1]
    onehot = (flat == lax.broadcasted_iota(jnp.int32, (experts, pairs), 0)).astype(BF)
    earlier = lax.broadcasted_iota(jnp.int32, (pairs, pairs), 0) < lax.broadcasted_iota(
        jnp.int32, (pairs, pairs), 1
    )
    before = dot(onehot, earlier.astype(BF), ((1,), (0,)))
    place = jnp.sum(before * onehot.astype(F32), axis=0).astype(jnp.int32)
    return place.reshape(routes_t.shape)


def width_sum(partial, mask):
    parts = lax.all_to_all(partial.astype(BF), WIDTH, 0, 0)
    total = jnp.sum(parts.astype(F32), axis=0)
    mine = (total * mask).astype(BF)
    return lax.all_gather(mine, WIDTH)


def pad_cols(a):
    return jnp.pad(a, ((0, 0),) * (a.ndim - 1) + ((0, 2 * HALF - a.shape[-1]),))


def swap_y(a):
    return lax.ppermute(a, "yh", [(0, 1), (1, 0)])


def pair_kernel(target, gates, base, down, back, pg_out, mixed_out, summed_out, mixed_acc, summed_acc):
    step = pl.program_id(0)
    tile, tokens = back.shape[0], base.shape[0]
    ids = lax.broadcasted_iota(jnp.int32, (tile, tokens), 0) + step * tile
    pick = jnp.zeros((tile, tokens), F32)
    gate = jnp.zeros((tile, tokens), F32)
    for k in range(4):
        hit = target[k : k + 1, :] == ids
        pick = jnp.where(hit, 1.0, pick)
        gate = jnp.where(hit, gates[k : k + 1, :], gate)
    gate = jnp.sum(gate, axis=1, keepdims=True)
    pick = pick.astype(BF)
    pre = dot(pick, base[...], ((1,), (0,))) + back[...].astype(F32)
    pair_down = (gate * dot(pick, down[...], ((1,), (0,)))).astype(BF).astype(F32)
    act, up = pre[:, :HALF], pre[:, HALF:]
    sig = jax.nn.sigmoid(act)
    swish = act * sig
    weighted = (gate * (swish * up)).astype(BF)
    grad_act = (pair_down * up * sig * (1.0 + act * (1.0 - sig))).astype(BF)
    grad_up = (pair_down * swish).astype(BF)
    pg_out[:, :HALF] = grad_act
    pg_out[:, HALF:] = grad_up

    @pl.when(step == 0)
    def _():
        mixed_acc[...] = jnp.zeros_like(mixed_acc)
        summed_acc[...] = jnp.zeros_like(summed_acc)

    mixed_acc[...] += dot(pick, weighted, ((0,), (0,)))
    summed_acc[:, :HALF] += dot(pick, grad_act, ((0,), (0,)))
    summed_acc[:, HALF:] += dot(pick, grad_up, ((0,), (0,)))

    @pl.when(step == pl.num_programs(0) - 1)
    def _():
        mixed_out[...] = mixed_acc[...].astype(BF)
        summed_out[...] = summed_acc[...].astype(BF)


def pair_step(target, gates, base, down, back):
    slots, tokens, tile = back.shape[0], base.shape[0], 320

    def whole(a):
        return pl.BlockSpec(a.shape, lambda i: (0, 0))

    tiled = pl.BlockSpec((tile, 2 * HALF), lambda i: (i, 0))
    sums = [pl.BlockSpec((tokens, n * HALF), lambda i: (0, 0)) for n in (1, 2)]
    return pl.pallas_call(
        pair_kernel,
        grid=(slots // tile,),
        in_specs=[whole(target), whole(gates), whole(base), whole(down), tiled],
        out_specs=[tiled] + sums,
        out_shape=[
            jax.ShapeDtypeStruct((slots, 2 * HALF), BF),
            jax.ShapeDtypeStruct((tokens, HALF), BF),
            jax.ShapeDtypeStruct((tokens, 2 * HALF), BF),
        ],
        scratch_shapes=[pltpu.VMEM((tokens, HALF), F32), pltpu.VMEM((tokens, 2 * HALF), F32)],
        compiler_params=pltpu.CompilerParams(vmem_limit_bytes=40 * 2**20),
        cost_estimate=pl.CostEstimate(
            flops=4 * slots * tokens * 3 * HALF, bytes_accessed=5 * 2**20, transcendentals=slots * HALF
        ),
    )(target, gates, base, down, back)


def one_expert(shape):
    return pl.BlockSpec((1,) + shape[1:], lambda e: (e,) + (0,) * (len(shape) - 1))


def all_of(shape):
    return pl.BlockSpec(shape, lambda e: (0,) * len(shape))


def expert_call(kernel, ins, outs, scratch, flops):
    def spec(shape, split):
        return one_expert(shape) if split else all_of(shape)

    return pl.pallas_call(
        kernel,
        grid=(4,),
        in_specs=[spec(a.shape, split) for a, split in ins],
        out_specs=[spec(shape, split) for shape, split in outs],
        out_shape=[jax.ShapeDtypeStruct(shape, BF) for shape, _ in outs],
        scratch_shapes=scratch,
        compiler_params=pltpu.CompilerParams(vmem_limit_bytes=40 * 2**20),
        cost_estimate=pl.CostEstimate(flops=flops, bytes_accessed=12 * 2**20, transcendentals=0),
    )(*[a for a, _ in ins])


def expert_rows(rows):
    return pl.ds(pl.multiple_of(pl.program_id(0) * rows, 32), rows)


def low_kernel(arrived, perm, factor, rows_out, low_out):
    @pl.when(pl.program_id(0) == 0)
    def _():
        rows_out[...] = dot(perm[...], arrived[...], ((1,), (0,))).astype(BF)

    mine = rows_out[expert_rows(low_out.shape[1]), :]
    low_out[0] = dot(mine, factor[0], ((1,), (0,))).astype(BF)


def pre_kernel(low, factor, perm_t, out, cols):
    step = pl.program_id(0)

    @pl.when(step == 0)
    def _():
        cols[...] = jnp.zeros_like(cols)

    rows = expert_rows(low.shape[1])
    rest = factor.shape[2] - HALF
    for c in range(2):
        pre = dot(low[0], factor[0, c], ((1,), (1,))).astype(BF)
        cols[0, rows, c * HALF : (c + 1) * HALF] = pre[:, :HALF]
        cols[1, rows, c * HALF : c * HALF + rest] = pre[:, HALF:]

    @pl.when(step == pl.num_programs(0) - 1)
    def _():
        for h in range(2):
            out[h] = dot(perm_t[...], cols[h], ((1,), (0,))).astype(BF)


def grad_kernel(arrived, perm, factor, low_out, pg_out):
    @pl.when(pl.program_id(0) == 0)
    def _():
        for h in range(2):
            both = dot(perm[...], arrived[h], ((1,), (0,))).astype(BF)
            for c in range(2):
                pg_out[c, :, h * HALF : (h + 1) * HALF] = both[:, c * HALF : (c + 1) * HALF]

    rows = expert_rows(low_out.shape[1])
    part = factor.shape[2]
    total = dot(pg_out[0, rows, :part], factor[0, 0], ((1,), (0,)))
    total += dot(pg_out[1, rows, :part], factor[0, 1], ((1,), (0,)))
    low_out[0] = total.astype(BF)


def back_kernel(low_grad, factor, perm_t, out, cols):
    step = pl.program_id(0)
    rows = expert_rows(low_grad.shape[1])
    cols[rows, :] = dot(low_grad[0], factor[0], ((1,), (1,))).astype(BF)

    @pl.when(step == pl.num_programs(0) - 1)
    def _():
        out[...] = dot(perm_t[...], cols[...], ((1,), (0,))).astype(BF)


def after(value, first):
    return lax.optimization_barrier((value, first))[0]


def hop(v, axis, k):
    return lax.ppermute(v, axis, [(i, (i + k) % 4) for i in range(4)])


def ring_send(vs, axis, dim):
    at = lax.axis_index(axis)

    def entry(k):
        return jnp.concatenate(
            [lax.dynamic_index_in_dim(v, (at + k) % 4, dim, keepdims=False) for v in vs], axis=-1
        )

    return [entry(0), hop(entry(1), axis, 1), hop(entry(3), axis, 3), entry(2)]


def ring_rest(parts, axis, first=None):
    last = parts[3] if first is None else after(parts[3], first)
    return parts[:3] + [hop(last, axis, 2)]


def ring_total(parts, first):
    parts = after(parts, first)
    return sum((p.astype(F32) for p in parts[1:]), parts[0].astype(F32)).astype(BF)


def local(tokens, grad_out, routes, gates, ranks, w_gate, w_up, w_down, delta_in, delta_out):
    yh = lax.axis_index("yh")
    wi = lax.axis_index("yl") * 2 + lax.axis_index("c")
    rows, part = tokens.shape
    local_e, _, rank_max = delta_in.shape
    n_exp = 32
    experts = n_exp * local_e
    slots = experts * CAP
    er = n_exp * CAP
    wr = w_gate.shape[0]
    rest = part - HALF

    d_id = lax.broadcasted_iota(jnp.int32, (part, WPART), 0)
    j_id = lax.broadcasted_iota(jnp.int32, (part, WPART), 1)
    spread = ((d_id // wr == j_id // PADDED) & (d_id % wr == j_id % PADDED)).astype(BF)

    place = targets_of(routes.T, experts)
    routes_t, gates_t = routes.T, gates.T
    info = jnp.concatenate([(routes_t * 8 + place).astype(F32), gates_t], axis=0)
    target = (routes_t // local_e) * XROWS + (routes_t % local_e) * CAP + place
    slot_ids = lax.broadcasted_iota(jnp.int32, (n_exp * XROWS, rows), 0)
    picker = sum((target[k : k + 1] == slot_ids).astype(F32) for k in range(4)).astype(BF)

    out_x = dot(picker, tokens, ((1,), (0,))).astype(BF).reshape(n_exp, XROWS, part)
    in_x = lax.all_to_all(out_x, EXPERT, 0, 0).reshape(n_exp * XROWS, part)

    xy = jnp.stack([dot(tokens, spread, ((1,), (0,))), dot(grad_out, spread, ((1,), (0,)))]).astype(BF)
    core, low_y = lax.axis_index("c"), lax.axis_index("yl")
    swap = [(0, 1), (1, 0)]

    def pair_up(at, mine, theirs, axis):
        return jnp.where(
            at == 0, jnp.concatenate([mine, theirs], axis=axis), jnp.concatenate([theirs, mine], axis=axis)
        )

    xy_far = swap_y(after(xy, out_x))

    far = swap_y(after(info, out_x))
    w3 = jnp.stack([pad_cols(w_gate), pad_cols(w_up), pad_cols(w_down.T)], axis=1)
    w3 = jnp.pad(w3, ((0, PADDED - wr), (0, 0), (0, 0)))
    keep = lax.dynamic_slice_in_dim(w3, yh * HALF, HALF, 2).reshape(PADDED, 3 * HALF)
    give = lax.dynamic_slice_in_dim(w3, (1 - yh) * HALF, HALF, 2).reshape(PADDED, 3 * HALF)
    both_w = lax.all_gather(after(jnp.stack([keep, swap_y(give)]), out_x), PLANE)
    own_w, far_w = [both_w[:, i].reshape(2 * WPART, 3 * HALF) for i in range(2)]

    def order(width, source):
        r = lax.broadcasted_iota(jnp.int32, (slots, width), 0)
        s_in = lax.broadcasted_iota(jnp.int32, (slots, width), 1)
        return (s_in == source(r // er, (r % er) // (2 * CAP), (r % (2 * CAP)) // CAP, r % CAP)).astype(BF)

    perm_x = order(n_exp * XROWS, lambda e, zx, b, p: (b * 16 + zx) * XROWS + e * CAP + p)
    perm_p = order(slots, lambda e, zx, b, p: (zx * 2 + b) * (local_e * CAP) + e * CAP + p)
    factor_out = delta_out.transpose(0, 2, 3, 1)
    rows_x, low_part = expert_call(
        low_kernel,
        [(in_x, False), (perm_x, False), (delta_in, True)],
        [((slots, part), False), ((local_e, er, rank_max), True)],
        [],
        12 * 10**8,
    )
    rows_x = rows_x.reshape(local_e, er, part)
    xy, xy_far = after((xy, xy_far), low_part)
    near = pair_up(yh, xy, xy_far, 1)
    across = lax.ppermute(near, "yl", swap)
    rank_ids = lax.broadcasted_iota(jnp.int32, (1, rank_max), 1)
    mask = (rank_ids < ranks[wi]).astype(F32)
    low = width_sum(low_part, mask)
    [out_pre] = expert_call(
        pre_kernel,
        [(low, True), (factor_out, True), (perm_p.T, False)],
        [((2, slots, 2 * HALF), False)],
        [pltpu.VMEM((2, slots, 2 * HALF), BF)],
        22 * 10**8,
    )
    far = after(far, (both_w, out_pre))
    info2 = jnp.where(
        yh == 0, jnp.concatenate([info, far], axis=1), jnp.concatenate([far, info], axis=1)
    )
    near, across = after((near, across), (both_w, out_pre))
    at_own = low_y == yh
    parts = jnp.stack([jnp.where(at_own, near, across), jnp.where(at_own, across, near)])
    parts = pair_up(core, parts, lax.ppermute(parts, "c", swap), 3)
    own_x, own_y, far_x, far_y = parts[0, 0], parts[0, 1], parts[1, 0], parts[1, 1]
    back_pre = lax.all_to_all(out_pre.reshape(n_exp, 2 * local_e * CAP, 2 * HALF), EXPERT, 0, 0)
    back_pre = back_pre.reshape(2 * slots, 2 * HALF)

    coded = info2[:4].astype(jnp.int32)
    route2, place2 = coded // 8, coded % 8
    block2 = lax.broadcasted_iota(jnp.int32, (4, 2 * rows), 1) // rows
    target2 = ((route2 // local_e) * 2 + block2) * (local_e * CAP) + (route2 % local_e) * CAP + place2

    own_gu, own_d, far_gu, far_d = own_w[:, : 2 * HALF], own_w[:, 2 * HALF :], far_w[:, : 2 * HALF], far_w[:, 2 * HALF :]
    base = (dot(own_x, own_gu, ((1,), (0,))) + dot(far_x, far_gu, ((1,), (0,)))).astype(BF)
    down = (dot(own_y, own_d, ((1,), (0,))) + dot(far_y, far_d, ((1,), (0,)))).astype(BF)
    pair_grad, mixed, summed = pair_step(target2, info2[4:], base, down, back_pre)
    in_p = lax.all_to_all(pair_grad.reshape(n_exp, 2 * local_e * CAP, 2 * HALF), EXPERT, 0, 0)
    in_p = in_p.reshape(2, slots, 2 * HALF)

    def plane_send(feats, axis):
        dws = [
            dot(f, g, ((0,), (0,))).astype(BF).reshape(4, 4, PADDED, -1) for f, g in zip(feats, (summed, mixed))
        ]
        return ring_send(dws, axis, 1 if axis == "x" else 0)

    low_back, pg = expert_call(
        grad_kernel,
        [(in_p, False), (perm_p, False), (factor_out, True)],
        [((local_e, er, rank_max), True), ((2, slots, 2 * HALF), False)],
        [],
        22 * 10**8,
    )
    far_parts = plane_send((far_x, far_y), "x")
    own_parts = plane_send((own_x, own_y), "z")
    low_back = after(low_back, (far_parts[1], far_parts[2], own_parts[1], own_parts[2]))
    far_parts, own_parts = ring_rest(far_parts, "x", low_back), ring_rest(own_parts, "z", low_back)

    def dx_part(w, at):
        w_at = lax.dynamic_slice_in_dim(w, at * WPART, WPART, 0)[:, : 2 * HALF]
        return dot(summed, w_at, ((1,), (1,))).astype(BF)

    dx_core = (
        jnp.stack([dx_part(w, core) for w in (own_w, far_w)]),
        lax.ppermute(jnp.stack([dx_part(w, 1 - core) for w in (own_w, far_w)]), "c", swap),
    )
    dx_core = after(dx_core, low_back)
    dx_own, dx_far = [(dx_core[0][i].astype(F32) + dx_core[1][i].astype(F32)).astype(BF) for i in range(2)]
    dx_keep, dx_give = jnp.where(at_own, dx_own, dx_far), jnp.where(at_own, dx_far, dx_own)
    dx_got = lax.ppermute(dx_give, "yl", swap)

    low_grad = width_sum(low_back, mask)
    [back] = expert_call(
        back_kernel,
        [(low_grad, True), (delta_in, True), (perm_x.T, False)],
        [((n_exp * XROWS, part), False)],
        [pltpu.VMEM((slots, part), BF)],
        12 * 10**8,
    )
    far_parts = ring_rest(ring_send([ring_total(far_parts, back)], "z", 0), "z")
    own_parts = ring_rest(ring_send([ring_total(own_parts, back)], "x", 0), "x")
    sums_done = (far_parts[0], own_parts[0])
    pg = after(pg, sums_done).reshape(2, local_e, er, 2 * HALF)[..., :part]
    grad_delta_out = lax.dot_general(
        low, pg, (((1,), (2,)), ((0,), (1,))), preferred_element_type=F32
    ).astype(BF)
    grad_delta_in = bdot(after(rows_x, sums_done), low_grad, ((1,), (1,))).astype(BF)
    dx_keep, dx_got = after((dx_keep, dx_got), back)
    dx = (dx_keep.astype(F32) + dx_got.astype(F32)).astype(BF)
    dx_keep = lax.dynamic_slice_in_dim(dx, yh * rows, rows, 0)
    dx_give = lax.dynamic_slice_in_dim(dx, (1 - yh) * rows, rows, 0)
    dx = dx_keep.astype(F32) + swap_y(dx_give).astype(F32)
    dx_hi = dx.astype(BF)
    dx_lo = (dx - dx_hi.astype(F32)).astype(BF)
    token_grad = dot(dx_hi, spread, ((1,), (1,))) + dot(dx_lo, spread, ((1,), (1,)))

    other = swap_y(ring_total(far_parts, back))
    mine = ring_total(own_parts, back)
    lo = jnp.where(yh == 0, mine, other)[:wr]
    hi = jnp.where(yh == 0, other, mine)[:wr]
    grads = [
        jnp.concatenate([lo[:, i * HALF : (i + 1) * HALF], hi[:, i * HALF : i * HALF + rest]], axis=1)
        for i in range(3)
    ]
    back = lax.all_to_all(back.reshape(n_exp, XROWS, part), EXPERT, 0, 0).reshape(n_exp * XROWS, part)
    grad_tokens = (token_grad + dot(picker, back, ((0,), (0,)))).astype(BF)
    return (grad_tokens, grads[0], grads[1], grads[2].T, grad_delta_in, grad_delta_out)


def solution(mesh):
    fine = Mesh(mesh.devices.reshape(2, 4, 4, 2, 2), ("yh", "z", "x", "yl", "c"))
    return jax.shard_map(
        local,
        mesh=fine,
        in_specs=(
            P(EXPERT, WIDTH),
            P(EXPERT, WIDTH),
            P(EXPERT, None),
            P(EXPERT, None),
            P(EXPERT),
            P(EXPERT, WIDTH),
            P(EXPERT, WIDTH),
            P(WIDTH, EXPERT),
            P(EXPERT, WIDTH, None),
            P(EXPERT, None, None, WIDTH),
        ),
        out_specs=(
            P(EXPERT, WIDTH),
            P(EXPERT, WIDTH),
            P(EXPERT, WIDTH),
            P(WIDTH, EXPERT),
            P(EXPERT, WIDTH, None),
            P(EXPERT, None, None, WIDTH),
        ),
        check_vma=False,
    )
```

```python
import jax
import jax.numpy as jnp
from jax import lax
from jax.experimental import pallas as pl
from jax.experimental.pallas import tpu as pltpu
from jax.sharding import Mesh, PartitionSpec as P

BF = jnp.bfloat16
F32 = jnp.float32
EXPERT = ("yh", "z", "x")
PLANE = ("z", "x")
WIDTH = ("yl", "c")
CAP = 5
HALF = 384
PADDED = 96
WPART = 768
XROWS = 24


def dot(a, b, dims):
    return lax.dot_general(a, b, (dims, ((), ())), preferred_element_type=F32)


def bdot(a, b, dims):
    return lax.dot_general(a, b, (dims, ((0,), (0,))), preferred_element_type=F32)


def targets_of(routes_t, experts):
    flat = routes_t.reshape(1, -1)
    pairs = flat.shape[1]
    onehot = (flat == lax.broadcasted_iota(jnp.int32, (experts, pairs), 0)).astype(BF)
    earlier = lax.broadcasted_iota(jnp.int32, (pairs, pairs), 0) < lax.broadcasted_iota(
        jnp.int32, (pairs, pairs), 1
    )
    before = dot(onehot, earlier.astype(BF), ((1,), (0,)))
    place = jnp.sum(before * onehot.astype(F32), axis=0).astype(jnp.int32)
    return place.reshape(routes_t.shape)


def width_sum(partial, mask):
    parts = lax.all_to_all(partial.astype(BF), WIDTH, 0, 0)
    total = jnp.sum(parts.astype(F32), axis=0)
    mine = (total * mask).astype(BF)
    return lax.all_gather(mine, WIDTH)


def pad_cols(a):
    return jnp.pad(a, ((0, 0),) * (a.ndim - 1) + ((0, 2 * HALF - a.shape[-1]),))


def swap_y(a):
    return lax.ppermute(a, "yh", [(0, 1), (1, 0)])


def pair_kernel(target, gates, base, down, back, pg_out, mixed_out, summed_out, mixed_acc, summed_acc):
    step = pl.program_id(0)
    tile, tokens = back.shape[0], base.shape[0]
    ids = lax.broadcasted_iota(jnp.int32, (tile, tokens), 0) + step * tile
    pick = jnp.zeros((tile, tokens), F32)
    gate = jnp.zeros((tile, tokens), F32)
    for k in range(4):
        hit = target[k : k + 1, :] == ids
        pick = jnp.where(hit, 1.0, pick)
        gate = jnp.where(hit, gates[k : k + 1, :], gate)
    gate = jnp.sum(gate, axis=1, keepdims=True)
    pick = pick.astype(BF)
    pre = dot(pick, base[...], ((1,), (0,))) + back[...].astype(F32)
    pair_down = (gate * dot(pick, down[...], ((1,), (0,)))).astype(BF).astype(F32)
    act, up = pre[:, :HALF], pre[:, HALF:]
    sig = jax.nn.sigmoid(act)
    swish = act * sig
    weighted = (gate * (swish * up)).astype(BF)
    grad_act = (pair_down * up * sig * (1.0 + act * (1.0 - sig))).astype(BF)
    grad_up = (pair_down * swish).astype(BF)
    pg_out[:, :HALF] = grad_act
    pg_out[:, HALF:] = grad_up

    @pl.when(step == 0)
    def _():
        mixed_acc[...] = jnp.zeros_like(mixed_acc)
        summed_acc[...] = jnp.zeros_like(summed_acc)

    mixed_acc[...] += dot(pick, weighted, ((0,), (0,)))
    summed_acc[:, :HALF] += dot(pick, grad_act, ((0,), (0,)))
    summed_acc[:, HALF:] += dot(pick, grad_up, ((0,), (0,)))

    @pl.when(step == pl.num_programs(0) - 1)
    def _():
        mixed_out[...] = mixed_acc[...].astype(BF)
        summed_out[...] = summed_acc[...].astype(BF)


def pair_step(target, gates, base, down, back):
    slots, tokens, tile = back.shape[0], base.shape[0], 320

    def whole(a):
        return pl.BlockSpec(a.shape, lambda i: (0, 0))

    tiled = pl.BlockSpec((tile, 2 * HALF), lambda i: (i, 0))
    sums = [pl.BlockSpec((tokens, n * HALF), lambda i: (0, 0)) for n in (1, 2)]
    return pl.pallas_call(
        pair_kernel,
        grid=(slots // tile,),
        in_specs=[whole(target), whole(gates), whole(base), whole(down), tiled],
        out_specs=[tiled] + sums,
        out_shape=[
            jax.ShapeDtypeStruct((slots, 2 * HALF), BF),
            jax.ShapeDtypeStruct((tokens, HALF), BF),
            jax.ShapeDtypeStruct((tokens, 2 * HALF), BF),
        ],
        scratch_shapes=[pltpu.VMEM((tokens, HALF), F32), pltpu.VMEM((tokens, 2 * HALF), F32)],
        compiler_params=pltpu.CompilerParams(vmem_limit_bytes=40 * 2**20),
        cost_estimate=pl.CostEstimate(
            flops=4 * slots * tokens * 3 * HALF, bytes_accessed=5 * 2**20, transcendentals=slots * HALF
        ),
    )(target, gates, base, down, back)


def one_expert(shape):
    return pl.BlockSpec((1,) + shape[1:], lambda e: (e,) + (0,) * (len(shape) - 1))


def all_of(shape):
    return pl.BlockSpec(shape, lambda e: (0,) * len(shape))


def expert_call(kernel, ins, outs, scratch, flops):
    def spec(shape, split):
        return one_expert(shape) if split else all_of(shape)

    return pl.pallas_call(
        kernel,
        grid=(4,),
        in_specs=[spec(a.shape, split) for a, split in ins],
        out_specs=[spec(shape, split) for shape, split in outs],
        out_shape=[jax.ShapeDtypeStruct(shape, BF) for shape, _ in outs],
        scratch_shapes=scratch,
        compiler_params=pltpu.CompilerParams(vmem_limit_bytes=40 * 2**20),
        cost_estimate=pl.CostEstimate(flops=flops, bytes_accessed=12 * 2**20, transcendentals=0),
    )(*[a for a, _ in ins])


def expert_rows(rows):
    return pl.ds(pl.multiple_of(pl.program_id(0) * rows, 32), rows)


def low_kernel(arrived, perm, factor, rows_out, low_out):
    @pl.when(pl.program_id(0) == 0)
    def _():
        rows_out[...] = dot(perm[...], arrived[...], ((1,), (0,))).astype(BF)

    mine = rows_out[expert_rows(low_out.shape[1]), :]
    low_out[0] = dot(mine, factor[0], ((1,), (0,))).astype(BF)


def pre_kernel(low, factor, perm_t, out, cols):
    step = pl.program_id(0)

    @pl.when(step == 0)
    def _():
        cols[...] = jnp.zeros_like(cols)

    rows = expert_rows(low.shape[1])
    rest = factor.shape[2] - HALF
    for c in range(2):
        pre = dot(low[0], factor[0, c], ((1,), (1,))).astype(BF)
        cols[0, rows, c * HALF : (c + 1) * HALF] = pre[:, :HALF]
        cols[1, rows, c * HALF : c * HALF + rest] = pre[:, HALF:]

    @pl.when(step == pl.num_programs(0) - 1)
    def _():
        for h in range(2):
            out[h] = dot(perm_t[...], cols[h], ((1,), (0,))).astype(BF)


def grad_kernel(arrived, perm, factor, low_out, pg_out):
    @pl.when(pl.program_id(0) == 0)
    def _():
        for h in range(2):
            both = dot(perm[...], arrived[h], ((1,), (0,))).astype(BF)
            for c in range(2):
                pg_out[c, :, h * HALF : (h + 1) * HALF] = both[:, c * HALF : (c + 1) * HALF]

    rows = expert_rows(low_out.shape[1])
    part = factor.shape[2]
    total = dot(pg_out[0, rows, :part], factor[0, 0], ((1,), (0,)))
    total += dot(pg_out[1, rows, :part], factor[0, 1], ((1,), (0,)))
    low_out[0] = total.astype(BF)


def back_kernel(low_grad, factor, perm_t, out, cols):
    step = pl.program_id(0)
    rows = expert_rows(low_grad.shape[1])
    cols[rows, :] = dot(low_grad[0], factor[0], ((1,), (1,))).astype(BF)

    @pl.when(step == pl.num_programs(0) - 1)
    def _():
        out[...] = dot(perm_t[...], cols[...], ((1,), (0,))).astype(BF)


def after(value, first):
    return lax.optimization_barrier((value, first))[0]


def hop(v, axis, k):
    return lax.ppermute(v, axis, [(i, (i + k) % 4) for i in range(4)])


def ring_send(vs, axis, dim):
    at = lax.axis_index(axis)

    def entry(k):
        return jnp.concatenate(
            [lax.dynamic_index_in_dim(v, (at + k) % 4, dim, keepdims=False) for v in vs], axis=-1
        )

    return [entry(0), hop(entry(1), axis, 1), hop(entry(3), axis, 3), entry(2)]


def ring_rest(parts, axis, first=None):
    last = parts[3] if first is None else after(parts[3], first)
    return parts[:3] + [hop(last, axis, 2)]


def ring_total(parts, first):
    parts = after(parts, first)
    return sum((p.astype(F32) for p in parts[1:]), parts[0].astype(F32)).astype(BF)


def local(tokens, grad_out, routes, gates, ranks, w_gate, w_up, w_down, delta_in, delta_out):
    yh = lax.axis_index("yh")
    wi = lax.axis_index("yl") * 2 + lax.axis_index("c")
    rows, part = tokens.shape
    local_e, _, rank_max = delta_in.shape
    n_exp = 32
    experts = n_exp * local_e
    slots = experts * CAP
    er = n_exp * CAP
    wr = w_gate.shape[0]
    rest = part - HALF

    d_id = lax.broadcasted_iota(jnp.int32, (part, WPART), 0)
    j_id = lax.broadcasted_iota(jnp.int32, (part, WPART), 1)
    spread = ((d_id // wr == j_id // PADDED) & (d_id % wr == j_id % PADDED)).astype(BF)

    place = targets_of(routes.T, experts)
    routes_t, gates_t = routes.T, gates.T
    info = jnp.concatenate([(routes_t * 8 + place).astype(F32), gates_t], axis=0)
    target = (routes_t // local_e) * XROWS + (routes_t % local_e) * CAP + place
    slot_ids = lax.broadcasted_iota(jnp.int32, (n_exp * XROWS, rows), 0)
    picker = sum((target[k : k + 1] == slot_ids).astype(F32) for k in range(4)).astype(BF)

    xy = jnp.stack([dot(tokens, spread, ((1,), (0,))), dot(grad_out, spread, ((1,), (0,)))]).astype(BF)
    core, low_y = lax.axis_index("c"), lax.axis_index("yl")
    swap = [(0, 1), (1, 0)]

    def pair_up(at, mine, theirs, axis):
        return jnp.where(
            at == 0, jnp.concatenate([mine, theirs], axis=axis), jnp.concatenate([theirs, mine], axis=axis)
        )

    near = pair_up(yh, xy, swap_y(xy), 1)
    across = lax.ppermute(near, "yl", swap)
    at_own = low_y == yh
    parts = jnp.stack([jnp.where(at_own, near, across), jnp.where(at_own, across, near)])
    parts = pair_up(core, parts, lax.ppermute(parts, "c", swap), 3)
    own_x, own_y, far_x, far_y = parts[0, 0], parts[0, 1], parts[1, 0], parts[1, 1]

    out_x = dot(picker, tokens, ((1,), (0,))).astype(BF).reshape(n_exp, XROWS, part)
    out_x = after(out_x, near)
    in_x = lax.all_to_all(out_x, EXPERT, 0, 0).reshape(n_exp * XROWS, part)

    far = swap_y(after(info, out_x))
    info2 = jnp.where(
        yh == 0, jnp.concatenate([info, far], axis=1), jnp.concatenate([far, info], axis=1)
    )

    w3 = jnp.stack([pad_cols(w_gate), pad_cols(w_up), pad_cols(w_down.T)], axis=1)
    w3 = jnp.pad(w3, ((0, PADDED - wr), (0, 0), (0, 0)))
    keep = lax.dynamic_slice_in_dim(w3, yh * HALF, HALF, 2).reshape(PADDED, 3 * HALF)
    give = lax.dynamic_slice_in_dim(w3, (1 - yh) * HALF, HALF, 2).reshape(PADDED, 3 * HALF)
    both_w = lax.all_gather(after(jnp.stack([keep, swap_y(give)]), out_x), PLANE)
    own_w, far_w = [both_w[:, i].reshape(2 * WPART, 3 * HALF) for i in range(2)]

    def order(width, source):
        r = lax.broadcasted_iota(jnp.int32, (slots, width), 0)
        s_in = lax.broadcasted_iota(jnp.int32, (slots, width), 1)
        return (s_in == source(r // er, (r % er) // (2 * CAP), (r % (2 * CAP)) // CAP, r % CAP)).astype(BF)

    perm_x = order(n_exp * XROWS, lambda e, zx, b, p: (b * 16 + zx) * XROWS + e * CAP + p)
    perm_p = order(slots, lambda e, zx, b, p: (zx * 2 + b) * (local_e * CAP) + e * CAP + p)
    factor_out = delta_out.transpose(0, 2, 3, 1)
    rows_x, low_part = expert_call(
        low_kernel,
        [(in_x, False), (perm_x, False), (delta_in, True)],
        [((slots, part), False), ((local_e, er, rank_max), True)],
        [],
        12 * 10**8,
    )
    rows_x = rows_x.reshape(local_e, er, part)
    rank_ids = lax.broadcasted_iota(jnp.int32, (1, rank_max), 1)
    mask = (rank_ids < ranks[wi]).astype(F32)
    low = width_sum(low_part, mask)
    [out_pre] = expert_call(
        pre_kernel,
        [(low, True), (factor_out, True), (perm_p.T, False)],
        [((2, slots, 2 * HALF), False)],
        [pltpu.VMEM((2, slots, 2 * HALF), BF)],
        22 * 10**8,
    )
    back_pre = lax.all_to_all(out_pre.reshape(n_exp, 2 * local_e * CAP, 2 * HALF), EXPERT, 0, 0)
    back_pre = back_pre.reshape(2 * slots, 2 * HALF)

    coded = info2[:4].astype(jnp.int32)
    route2, place2 = coded // 8, coded % 8
    block2 = lax.broadcasted_iota(jnp.int32, (4, 2 * rows), 1) // rows
    target2 = ((route2 // local_e) * 2 + block2) * (local_e * CAP) + (route2 % local_e) * CAP + place2

    own_gu, own_d, far_gu, far_d = own_w[:, : 2 * HALF], own_w[:, 2 * HALF :], far_w[:, : 2 * HALF], far_w[:, 2 * HALF :]
    base = (dot(own_x, own_gu, ((1,), (0,))) + dot(far_x, far_gu, ((1,), (0,)))).astype(BF)
    down = (dot(own_y, own_d, ((1,), (0,))) + dot(far_y, far_d, ((1,), (0,)))).astype(BF)
    pair_grad, mixed, summed = pair_step(target2, info2[4:], base, down, back_pre)
    in_p = lax.all_to_all(pair_grad.reshape(n_exp, 2 * local_e * CAP, 2 * HALF), EXPERT, 0, 0)
    in_p = in_p.reshape(2, slots, 2 * HALF)

    def plane_send(feats, axis):
        dws = [
            dot(f, g, ((0,), (0,))).astype(BF).reshape(4, 4, PADDED, -1) for f, g in zip(feats, (summed, mixed))
        ]
        return ring_send(dws, axis, 1 if axis == "x" else 0)

    low_back, pg = expert_call(
        grad_kernel,
        [(in_p, False), (perm_p, False), (factor_out, True)],
        [((local_e, er, rank_max), True), ((2, slots, 2 * HALF), False)],
        [],
        22 * 10**8,
    )
    far_parts = plane_send((far_x, far_y), "x")
    own_parts = plane_send((own_x, own_y), "z")
    low_back = after(low_back, (far_parts[1], far_parts[2], own_parts[1], own_parts[2]))
    far_parts, own_parts = ring_rest(far_parts, "x", low_back), ring_rest(own_parts, "z", low_back)
    low_grad = width_sum(low_back, mask)
    [back] = expert_call(
        back_kernel,
        [(low_grad, True), (delta_in, True), (perm_x.T, False)],
        [((n_exp * XROWS, part), False)],
        [pltpu.VMEM((slots, part), BF)],
        12 * 10**8,
    )
    def dx_part(w, at):
        w_at = lax.dynamic_slice_in_dim(w, at * WPART, WPART, 0)[:, : 2 * HALF]
        return dot(summed, w_at, ((1,), (1,))).astype(BF)

    dx_core = (
        jnp.stack([dx_part(w, core) for w in (own_w, far_w)]),
        lax.ppermute(after(jnp.stack([dx_part(w, 1 - core) for w in (own_w, far_w)]), low_back), "c", swap),
    )
    dx_core = after(dx_core, low_grad)
    dx_own, dx_far = [(dx_core[0][i].astype(F32) + dx_core[1][i].astype(F32)).astype(BF) for i in range(2)]
    dx_keep, dx_give = jnp.where(at_own, dx_own, dx_far), jnp.where(at_own, dx_far, dx_own)
    dx_got = lax.ppermute(dx_give, "yl", swap)
    far_parts = ring_rest(ring_send([ring_total(far_parts, back)], "z", 0), "z")
    own_parts = ring_rest(ring_send([ring_total(own_parts, back)], "x", 0), "x", dx_got)
    sums_done = (far_parts[0], own_parts[0])
    pg = after(pg, sums_done).reshape(2, local_e, er, 2 * HALF)[..., :part]
    grad_delta_out = lax.dot_general(
        low, pg, (((1,), (2,)), ((0,), (1,))), preferred_element_type=F32
    ).astype(BF)
    grad_delta_in = bdot(after(rows_x, sums_done), low_grad, ((1,), (1,))).astype(BF)
    dx = (dx_keep.astype(F32) + dx_got.astype(F32)).astype(BF)
    dx_keep = lax.dynamic_slice_in_dim(dx, yh * rows, rows, 0)
    dx_give = lax.dynamic_slice_in_dim(dx, (1 - yh) * rows, rows, 0)
    dx = dx_keep.astype(F32) + swap_y(dx_give).astype(F32)
    dx_hi = dx.astype(BF)
    dx_lo = (dx - dx_hi.astype(F32)).astype(BF)
    token_grad = dot(dx_hi, spread, ((1,), (1,))) + dot(dx_lo, spread, ((1,), (1,)))

    other = swap_y(ring_total(far_parts, back))
    mine = ring_total(own_parts, back)
    lo = jnp.where(yh == 0, mine, other)[:wr]
    hi = jnp.where(yh == 0, other, mine)[:wr]
    grads = [
        jnp.concatenate([lo[:, i * HALF : (i + 1) * HALF], hi[:, i * HALF : i * HALF + rest]], axis=1)
        for i in range(3)
    ]
    back = lax.all_to_all(back.reshape(n_exp, XROWS, part), EXPERT, 0, 0).reshape(n_exp * XROWS, part)
    grad_tokens = (token_grad + dot(picker, back, ((0,), (0,)))).astype(BF)
    return (grad_tokens, grads[0], grads[1], grads[2].T, grad_delta_in, grad_delta_out)


def solution(mesh):
    fine = Mesh(mesh.devices.reshape(2, 4, 4, 2, 2), ("yh", "z", "x", "yl", "c"))
    return jax.shard_map(
        local,
        mesh=fine,
        in_specs=(
            P(EXPERT, WIDTH),
            P(EXPERT, WIDTH),
            P(EXPERT, None),
            P(EXPERT, None),
            P(EXPERT),
            P(EXPERT, WIDTH),
            P(EXPERT, WIDTH),
            P(WIDTH, EXPERT),
            P(EXPERT, WIDTH, None),
            P(EXPERT, None, None, WIDTH),
        ),
        out_specs=(
            P(EXPERT, WIDTH),
            P(EXPERT, WIDTH),
            P(EXPERT, WIDTH),
            P(WIDTH, EXPERT),
            P(EXPERT, WIDTH, None),
            P(EXPERT, None, None, WIDTH),
        ),
        check_vma=False,
    )
```

```python
import jax
import jax.numpy as jnp
from jax import lax
from jax.experimental import pallas as pl
from jax.experimental.pallas import tpu as pltpu
from jax.sharding import Mesh, PartitionSpec as P

BF = jnp.bfloat16
F32 = jnp.float32
EXPERT = ("yh", "z", "x")
PLANE = ("z", "x")
WIDTH = ("yl", "c")
CAP = 5
HALF = 384
PADDED = 96
WPART = 768
XROWS = 24


def dot(a, b, dims):
    return lax.dot_general(a, b, (dims, ((), ())), preferred_element_type=F32)


def bdot(a, b, dims):
    return lax.dot_general(a, b, (dims, ((0,), (0,))), preferred_element_type=F32)


def targets_of(routes_t, experts):
    flat = routes_t.reshape(1, -1)
    pairs = flat.shape[1]
    onehot = (flat == lax.broadcasted_iota(jnp.int32, (experts, pairs), 0)).astype(BF)
    earlier = lax.broadcasted_iota(jnp.int32, (pairs, pairs), 0) < lax.broadcasted_iota(
        jnp.int32, (pairs, pairs), 1
    )
    before = dot(onehot, earlier.astype(BF), ((1,), (0,)))
    place = jnp.sum(before * onehot.astype(F32), axis=0).astype(jnp.int32)
    return place.reshape(routes_t.shape)


def width_sum(partial, mask, first=None):
    parts = lax.all_to_all(partial.astype(BF), WIDTH, 0, 0)
    total = jnp.sum(parts.astype(F32), axis=0)
    mine = (total * mask).astype(BF)
    if first is not None:
        mine = after(mine, first)
    return lax.all_gather(mine, WIDTH)


def pad_cols(a):
    return jnp.pad(a, ((0, 0),) * (a.ndim - 1) + ((0, 2 * HALF - a.shape[-1]),))


def swap_y(a):
    return lax.ppermute(a, "yh", [(0, 1), (1, 0)])


def pair_kernel(target, gates, base, down, back, pg_out, mixed_out, summed_out, mixed_acc, summed_acc):
    step = pl.program_id(0)
    tile, tokens = back.shape[0], base.shape[0]
    ids = lax.broadcasted_iota(jnp.int32, (tile, tokens), 0) + step * tile
    pick = jnp.zeros((tile, tokens), F32)
    gate = jnp.zeros((tile, tokens), F32)
    for k in range(4):
        hit = target[k : k + 1, :] == ids
        pick = jnp.where(hit, 1.0, pick)
        gate = jnp.where(hit, gates[k : k + 1, :], gate)
    gate = jnp.sum(gate, axis=1, keepdims=True)
    pick = pick.astype(BF)
    pre = dot(pick, base[...], ((1,), (0,))) + back[...].astype(F32)
    pair_down = (gate * dot(pick, down[...], ((1,), (0,)))).astype(BF).astype(F32)
    act, up = pre[:, :HALF], pre[:, HALF:]
    sig = jax.nn.sigmoid(act)
    swish = act * sig
    weighted = (gate * (swish * up)).astype(BF)
    grad_act = (pair_down * up * sig * (1.0 + act * (1.0 - sig))).astype(BF)
    grad_up = (pair_down * swish).astype(BF)
    pg_out[:, :HALF] = grad_act
    pg_out[:, HALF:] = grad_up

    @pl.when(step == 0)
    def _():
        mixed_acc[...] = jnp.zeros_like(mixed_acc)
        summed_acc[...] = jnp.zeros_like(summed_acc)

    mixed_acc[...] += dot(pick, weighted, ((0,), (0,)))
    summed_acc[:, :HALF] += dot(pick, grad_act, ((0,), (0,)))
    summed_acc[:, HALF:] += dot(pick, grad_up, ((0,), (0,)))

    @pl.when(step == pl.num_programs(0) - 1)
    def _():
        mixed_out[...] = mixed_acc[...].astype(BF)
        summed_out[...] = summed_acc[...].astype(BF)


def pair_step(target, gates, base, down, back):
    slots, tokens, tile = back.shape[0], base.shape[0], 320

    def whole(a):
        return pl.BlockSpec(a.shape, lambda i: (0, 0))

    tiled = pl.BlockSpec((tile, 2 * HALF), lambda i: (i, 0))
    sums = [pl.BlockSpec((tokens, n * HALF), lambda i: (0, 0)) for n in (1, 2)]
    return pl.pallas_call(
        pair_kernel,
        grid=(slots // tile,),
        in_specs=[whole(target), whole(gates), whole(base), whole(down), tiled],
        out_specs=[tiled] + sums,
        out_shape=[
            jax.ShapeDtypeStruct((slots, 2 * HALF), BF),
            jax.ShapeDtypeStruct((tokens, HALF), BF),
            jax.ShapeDtypeStruct((tokens, 2 * HALF), BF),
        ],
        scratch_shapes=[pltpu.VMEM((tokens, HALF), F32), pltpu.VMEM((tokens, 2 * HALF), F32)],
        compiler_params=pltpu.CompilerParams(vmem_limit_bytes=40 * 2**20),
        cost_estimate=pl.CostEstimate(
            flops=4 * slots * tokens * 3 * HALF, bytes_accessed=5 * 2**20, transcendentals=slots * HALF
        ),
    )(target, gates, base, down, back)


def one_expert(shape):
    return pl.BlockSpec((1,) + shape[1:], lambda e: (e,) + (0,) * (len(shape) - 1))


def all_of(shape):
    return pl.BlockSpec(shape, lambda e: (0,) * len(shape))


def expert_call(kernel, ins, outs, scratch, flops):
    def spec(shape, split):
        return one_expert(shape) if split else all_of(shape)

    return pl.pallas_call(
        kernel,
        grid=(4,),
        in_specs=[spec(a.shape, split) for a, split in ins],
        out_specs=[spec(shape, split) for shape, split in outs],
        out_shape=[jax.ShapeDtypeStruct(shape, BF) for shape, _ in outs],
        scratch_shapes=scratch,
        compiler_params=pltpu.CompilerParams(vmem_limit_bytes=40 * 2**20),
        cost_estimate=pl.CostEstimate(flops=flops, bytes_accessed=12 * 2**20, transcendentals=0),
    )(*[a for a, _ in ins])


def expert_rows(rows):
    return pl.ds(pl.multiple_of(pl.program_id(0) * rows, 32), rows)


def low_kernel(arrived, perm, factor, rows_out, low_out):
    @pl.when(pl.program_id(0) == 0)
    def _():
        rows_out[...] = dot(perm[...], arrived[...], ((1,), (0,))).astype(BF)

    mine = rows_out[expert_rows(low_out.shape[1]), :]
    low_out[0] = dot(mine, factor[0], ((1,), (0,))).astype(BF)


def pre_kernel(low, factor, perm_t, out, cols):
    step = pl.program_id(0)

    @pl.when(step == 0)
    def _():
        cols[...] = jnp.zeros_like(cols)

    rows = expert_rows(low.shape[1])
    rest = factor.shape[2] - HALF
    for c in range(2):
        pre = dot(low[0], factor[0, c], ((1,), (1,))).astype(BF)
        cols[0, rows, c * HALF : (c + 1) * HALF] = pre[:, :HALF]
        cols[1, rows, c * HALF : c * HALF + rest] = pre[:, HALF:]

    @pl.when(step == pl.num_programs(0) - 1)
    def _():
        for h in range(2):
            out[h] = dot(perm_t[...], cols[h], ((1,), (0,))).astype(BF)


def grad_kernel(arrived, perm, factor, low_out, pg_out):
    @pl.when(pl.program_id(0) == 0)
    def _():
        for h in range(2):
            both = dot(perm[...], arrived[h], ((1,), (0,))).astype(BF)
            for c in range(2):
                pg_out[c, :, h * HALF : (h + 1) * HALF] = both[:, c * HALF : (c + 1) * HALF]

    rows = expert_rows(low_out.shape[1])
    part = factor.shape[2]
    total = dot(pg_out[0, rows, :part], factor[0, 0], ((1,), (0,)))
    total += dot(pg_out[1, rows, :part], factor[0, 1], ((1,), (0,)))
    low_out[0] = total.astype(BF)


def back_kernel(low_grad, factor, perm_t, out, cols):
    step = pl.program_id(0)
    rows = expert_rows(low_grad.shape[1])
    cols[rows, :] = dot(low_grad[0], factor[0], ((1,), (1,))).astype(BF)

    @pl.when(step == pl.num_programs(0) - 1)
    def _():
        out[...] = dot(perm_t[...], cols[...], ((1,), (0,))).astype(BF)


def after(value, first):
    return lax.optimization_barrier((value, first))[0]


def hop(v, axis, k):
    return lax.ppermute(v, axis, [(i, (i + k) % 4) for i in range(4)])


def ring_send(vs, axis, dim):
    at = lax.axis_index(axis)

    def entry(k):
        return jnp.concatenate(
            [lax.dynamic_index_in_dim(v, (at + k) % 4, dim, keepdims=False) for v in vs], axis=-1
        )

    return [entry(0), hop(entry(1), axis, 1), hop(entry(3), axis, 3), entry(2)]


def ring_rest(parts, axis, first=None):
    last = parts[3] if first is None else after(parts[3], first)
    return parts[:3] + [hop(last, axis, 2)]


def ring_total(parts, first):
    parts = after(parts, first)
    return sum((p.astype(F32) for p in parts[1:]), parts[0].astype(F32)).astype(BF)


def local(tokens, grad_out, routes, gates, ranks, w_gate, w_up, w_down, delta_in, delta_out):
    yh = lax.axis_index("yh")
    wi = lax.axis_index("yl") * 2 + lax.axis_index("c")
    rows, part = tokens.shape
    local_e, _, rank_max = delta_in.shape
    n_exp = 32
    experts = n_exp * local_e
    slots = experts * CAP
    er = n_exp * CAP
    wr = w_gate.shape[0]
    rest = part - HALF

    d_id = lax.broadcasted_iota(jnp.int32, (part, WPART), 0)
    j_id = lax.broadcasted_iota(jnp.int32, (part, WPART), 1)
    spread = ((d_id // wr == j_id // PADDED) & (d_id % wr == j_id % PADDED)).astype(BF)

    place = targets_of(routes.T, experts)
    routes_t, gates_t = routes.T, gates.T
    info = jnp.concatenate([(routes_t * 8 + place).astype(F32), gates_t], axis=0)
    target = (routes_t // local_e) * XROWS + (routes_t % local_e) * CAP + place
    slot_ids = lax.broadcasted_iota(jnp.int32, (n_exp * XROWS, rows), 0)
    picker = sum((target[k : k + 1] == slot_ids).astype(F32) for k in range(4)).astype(BF)

    out_x = dot(picker, tokens, ((1,), (0,))).astype(BF).reshape(n_exp, XROWS, part)
    in_x = lax.all_to_all(out_x, EXPERT, 0, 0).reshape(n_exp * XROWS, part)

    xy = jnp.stack([dot(tokens, spread, ((1,), (0,))), dot(grad_out, spread, ((1,), (0,)))]).astype(BF)
    core, low_y = lax.axis_index("c"), lax.axis_index("yl")
    swap = [(0, 1), (1, 0)]

    def pair_up(at, mine, theirs, axis):
        return jnp.where(
            at == 0, jnp.concatenate([mine, theirs], axis=axis), jnp.concatenate([theirs, mine], axis=axis)
        )

    near = pair_up(yh, xy, swap_y(after(xy, out_x)), 1)
    across = lax.ppermute(near, "yl", swap)
    in_x = after(in_x, near)

    far = swap_y(after(info, out_x))
    w3 = jnp.stack([pad_cols(w_gate), pad_cols(w_up), pad_cols(w_down.T)], axis=1)
    w3 = jnp.pad(w3, ((0, PADDED - wr), (0, 0), (0, 0)))
    keep = lax.dynamic_slice_in_dim(w3, yh * HALF, HALF, 2).reshape(PADDED, 3 * HALF)
    give = lax.dynamic_slice_in_dim(w3, (1 - yh) * HALF, HALF, 2).reshape(PADDED, 3 * HALF)
    both_w = lax.all_gather(after(jnp.stack([keep, swap_y(give)]), out_x), PLANE)
    own_w, far_w = [both_w[:, i].reshape(2 * WPART, 3 * HALF) for i in range(2)]

    def order(width, source):
        r = lax.broadcasted_iota(jnp.int32, (slots, width), 0)
        s_in = lax.broadcasted_iota(jnp.int32, (slots, width), 1)
        return (s_in == source(r // er, (r % er) // (2 * CAP), (r % (2 * CAP)) // CAP, r % CAP)).astype(BF)

    perm_x = order(n_exp * XROWS, lambda e, zx, b, p: (b * 16 + zx) * XROWS + e * CAP + p)
    perm_p = order(slots, lambda e, zx, b, p: (zx * 2 + b) * (local_e * CAP) + e * CAP + p)
    factor_out = delta_out.transpose(0, 2, 3, 1)
    rows_x, low_part = expert_call(
        low_kernel,
        [(in_x, False), (perm_x, False), (delta_in, True)],
        [((slots, part), False), ((local_e, er, rank_max), True)],
        [],
        12 * 10**8,
    )
    rows_x = rows_x.reshape(local_e, er, part)
    rank_ids = lax.broadcasted_iota(jnp.int32, (1, rank_max), 1)
    mask = (rank_ids < ranks[wi]).astype(F32)
    low = width_sum(low_part, mask, across)
    [out_pre] = expert_call(
        pre_kernel,
        [(low, True), (factor_out, True), (perm_p.T, False)],
        [((2, slots, 2 * HALF), False)],
        [pltpu.VMEM((2, slots, 2 * HALF), BF)],
        22 * 10**8,
    )
    far = after(far, (both_w, out_pre))
    info2 = jnp.where(
        yh == 0, jnp.concatenate([info, far], axis=1), jnp.concatenate([far, info], axis=1)
    )
    near, across = after((near, across), (both_w, out_pre))
    at_own = low_y == yh
    parts = jnp.stack([jnp.where(at_own, near, across), jnp.where(at_own, across, near)])
    parts = pair_up(core, parts, lax.ppermute(parts, "c", swap), 3)
    own_x, own_y, far_x, far_y = parts[0, 0], parts[0, 1], parts[1, 0], parts[1, 1]
    back_pre = lax.all_to_all(out_pre.reshape(n_exp, 2 * local_e * CAP, 2 * HALF), EXPERT, 0, 0)
    back_pre = back_pre.reshape(2 * slots, 2 * HALF)

    coded = info2[:4].astype(jnp.int32)
    route2, place2 = coded // 8, coded % 8
    block2 = lax.broadcasted_iota(jnp.int32, (4, 2 * rows), 1) // rows
    target2 = ((route2 // local_e) * 2 + block2) * (local_e * CAP) + (route2 % local_e) * CAP + place2

    own_gu, own_d, far_gu, far_d = own_w[:, : 2 * HALF], own_w[:, 2 * HALF :], far_w[:, : 2 * HALF], far_w[:, 2 * HALF :]
    base = (dot(own_x, own_gu, ((1,), (0,))) + dot(far_x, far_gu, ((1,), (0,)))).astype(BF)
    down = (dot(own_y, own_d, ((1,), (0,))) + dot(far_y, far_d, ((1,), (0,)))).astype(BF)
    pair_grad, mixed, summed = pair_step(target2, info2[4:], base, down, back_pre)
    in_p = lax.all_to_all(pair_grad.reshape(n_exp, 2 * local_e * CAP, 2 * HALF), EXPERT, 0, 0)
    in_p = in_p.reshape(2, slots, 2 * HALF)

    def plane_send(feats, axis):
        dws = [
            dot(f, g, ((0,), (0,))).astype(BF).reshape(4, 4, PADDED, -1) for f, g in zip(feats, (summed, mixed))
        ]
        return ring_send(dws, axis, 1 if axis == "x" else 0)

    low_back, pg = expert_call(
        grad_kernel,
        [(in_p, False), (perm_p, False), (factor_out, True)],
        [((local_e, er, rank_max), True), ((2, slots, 2 * HALF), False)],
        [],
        22 * 10**8,
    )
    far_parts = plane_send((far_x, far_y), "x")
    own_parts = plane_send((own_x, own_y), "z")
    low_back = after(low_back, (far_parts[1], far_parts[2], own_parts[1], own_parts[2]))
    far_parts, own_parts = ring_rest(far_parts, "x", low_back), ring_rest(own_parts, "z", low_back)
    low_grad = width_sum(low_back, mask)
    [back] = expert_call(
        back_kernel,
        [(low_grad, True), (delta_in, True), (perm_x.T, False)],
        [((n_exp * XROWS, part), False)],
        [pltpu.VMEM((slots, part), BF)],
        12 * 10**8,
    )
    def dx_part(w, at):
        w_at = lax.dynamic_slice_in_dim(w, at * WPART, WPART, 0)[:, : 2 * HALF]
        return dot(summed, w_at, ((1,), (1,))).astype(BF)

    dx_core = (
        jnp.stack([dx_part(w, core) for w in (own_w, far_w)]),
        lax.ppermute(after(jnp.stack([dx_part(w, 1 - core) for w in (own_w, far_w)]), low_back), "c", swap),
    )
    dx_core = after(dx_core, low_grad)
    dx_own, dx_far = [(dx_core[0][i].astype(F32) + dx_core[1][i].astype(F32)).astype(BF) for i in range(2)]
    dx_keep, dx_give = jnp.where(at_own, dx_own, dx_far), jnp.where(at_own, dx_far, dx_own)
    dx_got = lax.ppermute(dx_give, "yl", swap)
    far_parts = ring_rest(ring_send([ring_total(far_parts, back)], "z", 0), "z")
    own_parts = ring_rest(ring_send([ring_total(own_parts, back)], "x", 0), "x", dx_got)
    sums_done = (far_parts[0], own_parts[0])
    pg = after(pg, sums_done).reshape(2, local_e, er, 2 * HALF)[..., :part]
    grad_delta_out = lax.dot_general(
        low, pg, (((1,), (2,)), ((0,), (1,))), preferred_element_type=F32
    ).astype(BF)
    grad_delta_in = bdot(after(rows_x, sums_done), low_grad, ((1,), (1,))).astype(BF)
    dx = (dx_keep.astype(F32) + dx_got.astype(F32)).astype(BF)
    dx_keep = lax.dynamic_slice_in_dim(dx, yh * rows, rows, 0)
    dx_give = lax.dynamic_slice_in_dim(dx, (1 - yh) * rows, rows, 0)
    dx = dx_keep.astype(F32) + swap_y(dx_give).astype(F32)
    dx_hi = dx.astype(BF)
    dx_lo = (dx - dx_hi.astype(F32)).astype(BF)
    token_grad = dot(dx_hi, spread, ((1,), (1,))) + dot(dx_lo, spread, ((1,), (1,)))

    other = swap_y(ring_total(far_parts, back))
    mine = ring_total(own_parts, back)
    lo = jnp.where(yh == 0, mine, other)[:wr]
    hi = jnp.where(yh == 0, other, mine)[:wr]
    grads = [
        jnp.concatenate([lo[:, i * HALF : (i + 1) * HALF], hi[:, i * HALF : i * HALF + rest]], axis=1)
        for i in range(3)
    ]
    back = lax.all_to_all(back.reshape(n_exp, XROWS, part), EXPERT, 0, 0).reshape(n_exp * XROWS, part)
    grad_tokens = (token_grad + dot(picker, back, ((0,), (0,)))).astype(BF)
    return (grad_tokens, grads[0], grads[1], grads[2].T, grad_delta_in, grad_delta_out)


def solution(mesh):
    fine = Mesh(mesh.devices.reshape(2, 4, 4, 2, 2), ("yh", "z", "x", "yl", "c"))
    return jax.shard_map(
        local,
        mesh=fine,
        in_specs=(
            P(EXPERT, WIDTH),
            P(EXPERT, WIDTH),
            P(EXPERT, None),
            P(EXPERT, None),
            P(EXPERT),
            P(EXPERT, WIDTH),
            P(EXPERT, WIDTH),
            P(WIDTH, EXPERT),
            P(EXPERT, WIDTH, None),
            P(EXPERT, None, None, WIDTH),
        ),
        out_specs=(
            P(EXPERT, WIDTH),
            P(EXPERT, WIDTH),
            P(EXPERT, WIDTH),
            P(WIDTH, EXPERT),
            P(EXPERT, WIDTH, None),
            P(EXPERT, None, None, WIDTH),
        ),
        check_vma=False,
    )
```

```python
import jax
import jax.numpy as jnp
from jax import lax
from jax.experimental import pallas as pl
from jax.experimental.pallas import tpu as pltpu
from jax.sharding import Mesh, PartitionSpec as P

BF = jnp.bfloat16
F32 = jnp.float32
EXPERT = ("yh", "z", "x")
PLANE = ("z", "x")
WIDTH = ("yl", "c")
CAP = 5
HALF = 384
PADDED = 96
WPART = 768
XROWS = 24


def dot(a, b, dims):
    return lax.dot_general(a, b, (dims, ((), ())), preferred_element_type=F32)


def bdot(a, b, dims):
    return lax.dot_general(a, b, (dims, ((0,), (0,))), preferred_element_type=F32)


def targets_of(routes_t, experts):
    flat = routes_t.reshape(1, -1)
    pairs = flat.shape[1]
    onehot = (flat == lax.broadcasted_iota(jnp.int32, (experts, pairs), 0)).astype(BF)
    earlier = lax.broadcasted_iota(jnp.int32, (pairs, pairs), 0) < lax.broadcasted_iota(
        jnp.int32, (pairs, pairs), 1
    )
    before = dot(onehot, earlier.astype(BF), ((1,), (0,)))
    place = jnp.sum(before * onehot.astype(F32), axis=0).astype(jnp.int32)
    return place.reshape(routes_t.shape)


def width_sum(partial, mask, first=None):
    parts = lax.all_to_all(partial.astype(BF), WIDTH, 0, 0)
    total = jnp.sum(parts.astype(F32), axis=0)
    mine = (total * mask).astype(BF)
    if first is not None:
        mine = after(mine, first)
    return lax.all_gather(mine, WIDTH)


def pad_cols(a):
    return jnp.pad(a, ((0, 0),) * (a.ndim - 1) + ((0, 2 * HALF - a.shape[-1]),))


def swap_y(a):
    return lax.ppermute(a, "yh", [(0, 1), (1, 0)])


def pair_kernel(target, gates, base, down, back, pg_out, mixed_out, summed_out, mixed_acc, summed_acc):
    step = pl.program_id(0)
    tile, tokens = back.shape[0], base.shape[0]
    ids = lax.broadcasted_iota(jnp.int32, (tile, tokens), 0) + step * tile
    pick = jnp.zeros((tile, tokens), F32)
    gate = jnp.zeros((tile, tokens), F32)
    for k in range(4):
        hit = target[k : k + 1, :] == ids
        pick = jnp.where(hit, 1.0, pick)
        gate = jnp.where(hit, gates[k : k + 1, :], gate)
    gate = jnp.sum(gate, axis=1, keepdims=True)
    pick = pick.astype(BF)
    pre = dot(pick, base[...], ((1,), (0,))) + back[...].astype(F32)
    pair_down = (gate * dot(pick, down[...], ((1,), (0,)))).astype(BF).astype(F32)
    act, up = pre[:, :HALF], pre[:, HALF:]
    sig = jax.nn.sigmoid(act)
    swish = act * sig
    weighted = (gate * (swish * up)).astype(BF)
    grad_act = (pair_down * up * sig * (1.0 + act * (1.0 - sig))).astype(BF)
    grad_up = (pair_down * swish).astype(BF)
    pg_out[:, :HALF] = grad_act
    pg_out[:, HALF:] = grad_up

    @pl.when(step == 0)
    def _():
        mixed_acc[...] = jnp.zeros_like(mixed_acc)
        summed_acc[...] = jnp.zeros_like(summed_acc)

    mixed_acc[...] += dot(pick, weighted, ((0,), (0,)))
    summed_acc[:, :HALF] += dot(pick, grad_act, ((0,), (0,)))
    summed_acc[:, HALF:] += dot(pick, grad_up, ((0,), (0,)))

    @pl.when(step == pl.num_programs(0) - 1)
    def _():
        mixed_out[...] = mixed_acc[...].astype(BF)
        summed_out[...] = summed_acc[...].astype(BF)


def pair_step(target, gates, base, down, back):
    slots, tokens, tile = back.shape[0], base.shape[0], 320

    def whole(a):
        return pl.BlockSpec(a.shape, lambda i: (0, 0))

    tiled = pl.BlockSpec((tile, 2 * HALF), lambda i: (i, 0))
    sums = [pl.BlockSpec((tokens, n * HALF), lambda i: (0, 0)) for n in (1, 2)]
    return pl.pallas_call(
        pair_kernel,
        grid=(slots // tile,),
        in_specs=[whole(target), whole(gates), whole(base), whole(down), tiled],
        out_specs=[tiled] + sums,
        out_shape=[
            jax.ShapeDtypeStruct((slots, 2 * HALF), BF),
            jax.ShapeDtypeStruct((tokens, HALF), BF),
            jax.ShapeDtypeStruct((tokens, 2 * HALF), BF),
        ],
        scratch_shapes=[pltpu.VMEM((tokens, HALF), F32), pltpu.VMEM((tokens, 2 * HALF), F32)],
        compiler_params=pltpu.CompilerParams(vmem_limit_bytes=40 * 2**20),
        cost_estimate=pl.CostEstimate(
            flops=4 * slots * tokens * 3 * HALF, bytes_accessed=5 * 2**20, transcendentals=slots * HALF
        ),
    )(target, gates, base, down, back)


def one_expert(shape):
    return pl.BlockSpec((1,) + shape[1:], lambda e: (e,) + (0,) * (len(shape) - 1))


def all_of(shape):
    return pl.BlockSpec(shape, lambda e: (0,) * len(shape))


def expert_call(kernel, ins, outs, scratch, flops, vmem=40):
    def spec(shape, split):
        return one_expert(shape) if split else all_of(shape)

    return pl.pallas_call(
        kernel,
        grid=(4,),
        in_specs=[spec(a.shape, split) for a, split in ins],
        out_specs=[spec(shape, split) for shape, split in outs],
        out_shape=[jax.ShapeDtypeStruct(shape, BF) for shape, _ in outs],
        scratch_shapes=scratch,
        compiler_params=pltpu.CompilerParams(vmem_limit_bytes=vmem * 2**20),
        cost_estimate=pl.CostEstimate(flops=flops, bytes_accessed=12 * 2**20, transcendentals=0),
    )(*[a for a, _ in ins])


def expert_rows(rows):
    return pl.ds(pl.multiple_of(pl.program_id(0) * rows, 32), rows)


def low_kernel(arrived, perm, factor, rows_out, low_out):
    @pl.when(pl.program_id(0) == 0)
    def _():
        rows_out[...] = dot(perm[...], arrived[...], ((1,), (0,))).astype(BF)

    mine = rows_out[expert_rows(low_out.shape[1]), :]
    low_out[0] = dot(mine, factor[0], ((1,), (0,))).astype(BF)


def pre_kernel(low, factor, perm_t, out, cols):
    step = pl.program_id(0)

    @pl.when(step == 0)
    def _():
        cols[...] = jnp.zeros_like(cols)

    rows = expert_rows(low.shape[1])
    rest = factor.shape[2] - HALF
    for c in range(2):
        pre = dot(low[0], factor[0, c], ((1,), (1,))).astype(BF)
        cols[0, rows, c * HALF : (c + 1) * HALF] = pre[:, :HALF]
        cols[1, rows, c * HALF : c * HALF + rest] = pre[:, HALF:]

    @pl.when(step == pl.num_programs(0) - 1)
    def _():
        for h in range(2):
            out[h] = dot(perm_t[...], cols[h], ((1,), (0,))).astype(BF)


def grad_kernel(arrived, perm, factor, low_out, pg_out):
    @pl.when(pl.program_id(0) == 0)
    def _():
        for h in range(2):
            both = dot(perm[...], arrived[h], ((1,), (0,))).astype(BF)
            for c in range(2):
                pg_out[c, :, h * HALF : (h + 1) * HALF] = both[:, c * HALF : (c + 1) * HALF]

    rows = expert_rows(low_out.shape[1])
    part = factor.shape[2]
    total = dot(pg_out[0, rows, :part], factor[0, 0], ((1,), (0,)))
    total += dot(pg_out[1, rows, :part], factor[0, 1], ((1,), (0,)))
    low_out[0] = total.astype(BF)


def back_kernel(low_grad, factor, perm_t, out, cols):
    step = pl.program_id(0)
    rows = expert_rows(low_grad.shape[1])
    cols[rows, :] = dot(low_grad[0], factor[0], ((1,), (1,))).astype(BF)

    @pl.when(step == pl.num_programs(0) - 1)
    def _():
        out[...] = dot(perm_t[...], cols[...], ((1,), (0,))).astype(BF)


def after(value, first):
    return lax.optimization_barrier((value, first))[0]


def hop(v, axis, k):
    return lax.ppermute(v, axis, [(i, (i + k) % 4) for i in range(4)])


def ring_send(vs, axis, dim):
    at = lax.axis_index(axis)

    def entry(k):
        return jnp.concatenate(
            [lax.dynamic_index_in_dim(v, (at + k) % 4, dim, keepdims=False) for v in vs], axis=-1
        )

    return [entry(0), hop(entry(1), axis, 1), hop(entry(3), axis, 3), entry(2)]


def ring_rest(parts, axis, first=None):
    last = parts[3] if first is None else after(parts[3], first)
    return parts[:3] + [hop(last, axis, 2)]


def ring_total(parts, first):
    parts = after(parts, first)
    return sum((p.astype(F32) for p in parts[1:]), parts[0].astype(F32)).astype(BF)


def local(tokens, grad_out, routes, gates, ranks, w_gate, w_up, w_down, delta_in, delta_out):
    yh = lax.axis_index("yh")
    wi = lax.axis_index("yl") * 2 + lax.axis_index("c")
    rows, part = tokens.shape
    local_e, _, rank_max = delta_in.shape
    n_exp = 32
    experts = n_exp * local_e
    slots = experts * CAP
    er = n_exp * CAP
    wr = w_gate.shape[0]
    rest = part - HALF

    d_id = lax.broadcasted_iota(jnp.int32, (part, WPART), 0)
    j_id = lax.broadcasted_iota(jnp.int32, (part, WPART), 1)
    spread = ((d_id // wr == j_id // PADDED) & (d_id % wr == j_id % PADDED)).astype(BF)

    place = targets_of(routes.T, experts)
    routes_t, gates_t = routes.T, gates.T
    info = jnp.concatenate([(routes_t * 8 + place).astype(F32), gates_t], axis=0)
    target = (routes_t // local_e) * XROWS + (routes_t % local_e) * CAP + place
    slot_ids = lax.broadcasted_iota(jnp.int32, (n_exp * XROWS, rows), 0)
    picker = sum((target[k : k + 1] == slot_ids).astype(F32) for k in range(4)).astype(BF)

    out_x = dot(picker, tokens, ((1,), (0,))).astype(BF).reshape(n_exp, XROWS, part)
    in_x = lax.all_to_all(out_x, EXPERT, 0, 0).reshape(n_exp * XROWS, part)

    xy = jnp.stack([dot(tokens, spread, ((1,), (0,))), dot(grad_out, spread, ((1,), (0,)))]).astype(BF)
    core, low_y = lax.axis_index("c"), lax.axis_index("yl")
    swap = [(0, 1), (1, 0)]

    def pair_up(at, mine, theirs, axis):
        return jnp.where(
            at == 0, jnp.concatenate([mine, theirs], axis=axis), jnp.concatenate([theirs, mine], axis=axis)
        )

    near = pair_up(yh, xy, swap_y(after(xy, out_x)), 1)
    across = lax.ppermute(near, "yl", swap)
    in_x = after(in_x, near)

    far = swap_y(after(info, out_x))
    w3 = jnp.stack([pad_cols(w_gate), pad_cols(w_up), pad_cols(w_down.T)], axis=1)
    w3 = jnp.pad(w3, ((0, PADDED - wr), (0, 0), (0, 0)))
    keep = lax.dynamic_slice_in_dim(w3, yh * HALF, HALF, 2).reshape(PADDED, 3 * HALF)
    give = lax.dynamic_slice_in_dim(w3, (1 - yh) * HALF, HALF, 2).reshape(PADDED, 3 * HALF)
    both_w = lax.all_gather(after(jnp.stack([keep, swap_y(give)]), out_x), PLANE)
    own_w, far_w = [both_w[:, i].reshape(2 * WPART, 3 * HALF) for i in range(2)]

    def order(width, source):
        r = lax.broadcasted_iota(jnp.int32, (slots, width), 0)
        s_in = lax.broadcasted_iota(jnp.int32, (slots, width), 1)
        return (s_in == source(r // er, (r % er) // (2 * CAP), (r % (2 * CAP)) // CAP, r % CAP)).astype(BF)

    perm_x = order(n_exp * XROWS, lambda e, zx, b, p: (b * 16 + zx) * XROWS + e * CAP + p)
    perm_p = order(slots, lambda e, zx, b, p: (zx * 2 + b) * (local_e * CAP) + e * CAP + p)
    factor_out = delta_out.transpose(0, 2, 3, 1)
    rows_x, low_part = expert_call(
        low_kernel,
        [(in_x, False), (perm_x, False), (delta_in, True)],
        [((slots, part), False), ((local_e, er, rank_max), True)],
        [],
        12 * 10**8,
    )
    rows_x = rows_x.reshape(local_e, er, part)
    rank_ids = lax.broadcasted_iota(jnp.int32, (1, rank_max), 1)
    mask = (rank_ids < ranks[wi]).astype(F32)
    low = width_sum(low_part, mask, across)
    [out_pre] = expert_call(
        pre_kernel,
        [(low, True), (factor_out, True), (perm_p.T, False)],
        [((2, slots, 2 * HALF), False)],
        [pltpu.VMEM((2, slots, 2 * HALF), BF)],
        22 * 10**8,
        56,
    )
    far = after(far, (both_w, out_pre))
    info2 = jnp.where(
        yh == 0, jnp.concatenate([info, far], axis=1), jnp.concatenate([far, info], axis=1)
    )
    near, across = after((near, across), (both_w, out_pre))
    at_own = low_y == yh
    parts = jnp.stack([jnp.where(at_own, near, across), jnp.where(at_own, across, near)])
    parts = pair_up(core, parts, lax.ppermute(parts, "c", swap), 3)
    own_x, own_y, far_x, far_y = parts[0, 0], parts[0, 1], parts[1, 0], parts[1, 1]
    back_pre = lax.all_to_all(out_pre.reshape(n_exp, 2 * local_e * CAP, 2 * HALF), EXPERT, 0, 0)
    back_pre = back_pre.reshape(2 * slots, 2 * HALF)

    coded = info2[:4].astype(jnp.int32)
    route2, place2 = coded // 8, coded % 8
    block2 = lax.broadcasted_iota(jnp.int32, (4, 2 * rows), 1) // rows
    target2 = ((route2 // local_e) * 2 + block2) * (local_e * CAP) + (route2 % local_e) * CAP + place2

    own_gu, own_d, far_gu, far_d = own_w[:, : 2 * HALF], own_w[:, 2 * HALF :], far_w[:, : 2 * HALF], far_w[:, 2 * HALF :]
    base = (dot(own_x, own_gu, ((1,), (0,))) + dot(far_x, far_gu, ((1,), (0,)))).astype(BF)
    down = (dot(own_y, own_d, ((1,), (0,))) + dot(far_y, far_d, ((1,), (0,)))).astype(BF)
    pair_grad, mixed, summed = pair_step(target2, info2[4:], base, down, back_pre)
    in_p = lax.all_to_all(pair_grad.reshape(n_exp, 2 * local_e * CAP, 2 * HALF), EXPERT, 0, 0)
    in_p = in_p.reshape(2, slots, 2 * HALF)

    def plane_send(feats, axis):
        dws = [
            dot(f, g, ((0,), (0,))).astype(BF).reshape(4, 4, PADDED, -1) for f, g in zip(feats, (summed, mixed))
        ]
        return ring_send(dws, axis, 1 if axis == "x" else 0)

    low_back, pg = expert_call(
        grad_kernel,
        [(in_p, False), (perm_p, False), (factor_out, True)],
        [((local_e, er, rank_max), True), ((2, slots, 2 * HALF), False)],
        [],
        22 * 10**8,
        56,
    )
    far_parts = plane_send((far_x, far_y), "x")
    own_parts = plane_send((own_x, own_y), "z")
    low_back = after(low_back, (far_parts[1], far_parts[2], own_parts[1], own_parts[2]))
    far_parts, own_parts = ring_rest(far_parts, "x", low_back), ring_rest(own_parts, "z", low_back)
    low_grad = width_sum(low_back, mask)
    [back] = expert_call(
        back_kernel,
        [(low_grad, True), (delta_in, True), (perm_x.T, False)],
        [((n_exp * XROWS, part), False)],
        [pltpu.VMEM((slots, part), BF)],
        12 * 10**8,
    )
    def dx_part(w, at):
        w_at = lax.dynamic_slice_in_dim(w, at * WPART, WPART, 0)[:, : 2 * HALF]
        return dot(summed, w_at, ((1,), (1,))).astype(BF)

    dx_core = (
        jnp.stack([dx_part(w, core) for w in (own_w, far_w)]),
        lax.ppermute(after(jnp.stack([dx_part(w, 1 - core) for w in (own_w, far_w)]), low_back), "c", swap),
    )
    dx_core = after(dx_core, low_grad)
    dx_own, dx_far = [(dx_core[0][i].astype(F32) + dx_core[1][i].astype(F32)).astype(BF) for i in range(2)]
    dx_keep, dx_give = jnp.where(at_own, dx_own, dx_far), jnp.where(at_own, dx_far, dx_own)
    dx_got = lax.ppermute(dx_give, "yl", swap)
    far_parts = ring_rest(ring_send([ring_total(far_parts, back)], "z", 0), "z")
    own_parts = ring_rest(ring_send([ring_total(own_parts, back)], "x", 0), "x", dx_got)
    sums_done = (far_parts[0], own_parts[0])
    pg = after(pg, sums_done).reshape(2, local_e, er, 2 * HALF)[..., :part]
    grad_delta_out = lax.dot_general(
        low, pg, (((1,), (2,)), ((0,), (1,))), preferred_element_type=F32
    ).astype(BF)
    grad_delta_in = bdot(after(rows_x, sums_done), low_grad, ((1,), (1,))).astype(BF)
    dx = (dx_keep.astype(F32) + dx_got.astype(F32)).astype(BF)
    dx_keep = lax.dynamic_slice_in_dim(dx, yh * rows, rows, 0)
    dx_give = lax.dynamic_slice_in_dim(dx, (1 - yh) * rows, rows, 0)
    dx = dx_keep.astype(F32) + swap_y(dx_give).astype(F32)
    dx_hi = dx.astype(BF)
    dx_lo = (dx - dx_hi.astype(F32)).astype(BF)
    token_grad = dot(dx_hi, spread, ((1,), (1,))) + dot(dx_lo, spread, ((1,), (1,)))

    other = swap_y(ring_total(far_parts, back))
    mine = ring_total(own_parts, back)
    lo = jnp.where(yh == 0, mine, other)[:wr]
    hi = jnp.where(yh == 0, other, mine)[:wr]
    grads = [
        jnp.concatenate([lo[:, i * HALF : (i + 1) * HALF], hi[:, i * HALF : i * HALF + rest]], axis=1)
        for i in range(3)
    ]
    back = lax.all_to_all(back.reshape(n_exp, XROWS, part), EXPERT, 0, 0).reshape(n_exp * XROWS, part)
    grad_tokens = (token_grad + dot(picker, back, ((0,), (0,)))).astype(BF)
    return (grad_tokens, grads[0], grads[1], grads[2].T, grad_delta_in, grad_delta_out)


def solution(mesh):
    fine = Mesh(mesh.devices.reshape(2, 4, 4, 2, 2), ("yh", "z", "x", "yl", "c"))
    return jax.shard_map(
        local,
        mesh=fine,
        in_specs=(
            P(EXPERT, WIDTH),
            P(EXPERT, WIDTH),
            P(EXPERT, None),
            P(EXPERT, None),
            P(EXPERT),
            P(EXPERT, WIDTH),
            P(EXPERT, WIDTH),
            P(WIDTH, EXPERT),
            P(EXPERT, WIDTH, None),
            P(EXPERT, None, None, WIDTH),
        ),
        out_specs=(
            P(EXPERT, WIDTH),
            P(EXPERT, WIDTH),
            P(EXPERT, WIDTH),
            P(WIDTH, EXPERT),
            P(EXPERT, WIDTH, None),
            P(EXPERT, None, None, WIDTH),
        ),
        check_vma=False,
    )
```
